32 devices in a mesh: gen: 2 (over x), learn: 16 (over z, y, core).
Axes of the slice: x: 2, y: 2, z: 4, core: 2. Of those that a mesh axis runs over, the one named last changes fastest.
Arguments:
- hidden: bfloat16 [8192, 5120], P(('gen', 'learn')), may hold values from -0.59765625 to 0.59765625
- cotangent: bfloat16 [8192, 1024], P(('gen', 'learn')), may hold values from -0.29882812 to 0.29882812
- importance: float32 [8192], P(('gen', 'learn')), may hold values from 0.25 to 4
- block_len: int32 [1024], P(('gen', 'learn')), may hold values from 1 to 8
- version: int32 [1024], P(('gen', 'learn')), may hold values from 0 to 3
- destination: int32 [1024, 1], P(('gen', 'learn')), may hold values from 0 to 15; in each aligned block of 32 rows (0 to 31, 32 to 63, ...) at most 4 rows name the same one
- w_key: bfloat16 [5120, 1024], replicated, may hold values from -0.078125 to 0.078125
- in_gain: float32 [5120], replicated, may hold values from 0.5 to 1.5
- key_gain: float32 [128], replicated, may hold values from 0.5 to 1.5
Outputs:
- grad_slots: bfloat16 [16384, 5120], P(('gen', 'learn'))
- w_grad: float32 [5120, 1024], P('gen')
- gain_grad: float32 [5120], replicated
- kgain_grad: float32 [128], replicated
The draws below stay inside these ranges and needn't reach their ends.
Inputs may be any that keep to these rules, and one draw needn't show every extreme that they name: `destination`: the 32 blocks of one device name each learner at most 4 times.
All inputs are finite; a program needn't handle non-finite values.
Results may differ from the reference program's by a relative error of at most 0.0075.
Values may be sent and summed in bfloat16 or wider, within the bound.
No kernel may reach another device: no remote copies, remote signals or barrier semaphores. Data moves between devices by JAX's collectives and lax.ppermute only.
A program may use at most 128 MiB of HBM per device.

```python
import math
import jax
import jax.numpy as jnp
import numpy as np
from jax import lax

D = 5120
HD = 128
TILE = 8
VERSIONS = 4
SLOTS = 64
TPS = 32
KD = 1024
CAP = 4
NT = 1024
N_GEN = 2
N_LEARN = 16


def touch_ends(result, stream_key, low, largest):
    shape = result.shape
    place = [jax.random.randint(jax.random.fold_in(stream_key, axis), (), 0, shape[axis]) for axis in range(len(shape))]
    result = result.at[tuple(place)].set(low)
    longest = shape.index(max(shape))
    place[longest] = (place[longest] + 1) % shape[longest]
    return result.at[tuple(place)].set(largest)


def steps_of(stream_key, dims, cuts, smallest, top_value):
    factor_of = 1.0
    for dim, shards_of in cuts:
        heights = jax.random.uniform(jax.random.fold_in(jax.random.fold_in(stream_key, 6), dim), (shards_of,), jnp.float32, smallest / len(cuts), top_value / len(cuts))
        factor_of = factor_of * jnp.repeat(jnp.exp(heights), dims[dim] // shards_of).reshape((-1,) + (1,) * (len(dims) - 1 - dim))
    return factor_of


def routed_block(rng, own, number, rows, amount, top, bound, skew):
    sequence = jax.random.permutation(rng, amount)
    crowded, common = portions_of(amount, rows * top, bound, skew, True), portions_of(amount, rows * top, bound, skew, False)
    places = jnp.arange(amount)

    def named(sizes, turn):
        used = int((sizes > 0).sum())
        fixed = max(1, used // 4)
        passed = fixed + (places - fixed + turn * (used - fixed)) % max(1, amount - fixed)
        return jnp.zeros((amount,), jnp.int32).at[sequence[jnp.where(places < fixed, places, passed)]].set(jnp.asarray(sizes, jnp.int32))

    sizes = jnp.where(number % 4 == 0, named(crowded, number // 4), named(common, number - number // 4 - 1))
    mixed = jax.random.permutation(jax.random.fold_in(own, 3), amount)
    source_of, receiver = mixed[0:amount // 2 * 2:2], mixed[1:amount // 2 * 2:2]
    slack = jnp.minimum(sizes[source_of] - 1, bound - sizes[receiver]) // 2
    slack = jnp.where((source_of == sequence[0]) | (receiver == sequence[0]) | (sizes[receiver] == 0), 0, jnp.maximum(slack, 0))
    passed = jax.random.randint(jax.random.fold_in(own, 4), (amount // 2,), 0, 1 << 20) % (slack + 1)
    sizes = sizes.at[source_of].add(-passed).at[receiver].add(passed)
    labels = jnp.searchsorted(jnp.cumsum(sizes), jnp.arange(rows * top), side="right").astype(jnp.int32)
    table = labels.reshape(top, rows).T
    table = table[jax.random.permutation(jax.random.fold_in(own, 1), rows)]
    turn = jax.random.randint(jax.random.fold_in(own, 2), (rows, 1), 0, top)
    return jnp.take_along_axis(table, (jnp.arange(top)[None, :] + turn) % top, axis=1)


def portions_of(amount, total, limit, slope, full):
    portions = [(1 << 20) // math.isqrt(rank ** slope) + 1 for rank in range(1, amount + 1)]
    largest = limit if full else min(limit, max(-(-total // amount), total * portions[0] // sum(portions)))
    least = 1 if total - largest >= amount - 1 else 0
    holding, spare = [largest] + [least] * (amount - 1), total - largest - least * (amount - 1)
    while spare > 0:
        free = [i for i in range(1, amount) if holding[i] < largest] or [i for i in range(1, amount) if holding[i] < limit]
        whole, budget = sum([portions[i] for i in free]), spare
        for i in free:
            addition = min(limit - holding[i], max(1, budget * portions[i] // whole), spare)
            holding[i] = holding[i] + addition
            spare = spare - addition
    return np.array(holding)


def noise(rng, dims, width, reach, shards=(), kind=jnp.bfloat16):
    factor_of = steps_of(rng, dims, shards, -0.22, 0.18) if shards else 1.0
    drawn = jax.random.normal(rng, dims, jnp.float32) * width * factor_of
    return jnp.minimum(jnp.maximum(drawn, -reach), reach).astype(kind)


def setup_inputs(seed: int = 0) -> dict:
    key_of = jax.random.split(jax.random.key(seed), 10)
    hidden = noise(key_of[0], (NT * TILE, D), 0.1, 0.59765625, ((0, 32),))
    cotangent = noise(key_of[1], (NT * TILE, KD), 0.05, 0.29882812, ((0, 32),))
    importance = jnp.clip(jnp.exp(math.log(4.0) - 2.7725887 * jax.random.uniform(key_of[2], (NT * TILE,), jnp.float32) ** steps_of(key_of[2], (NT * TILE,), ((0, 32),), -0.2, 0.2)), 0.25, 4.0)
    block_len = touch_ends(jax.random.randint(key_of[3], (NT,), 1, TILE + 1), jax.random.fold_in(key_of[3], 1), 1, TILE).astype(jnp.int32)
    version = touch_ends(jax.random.randint(key_of[4], (NT,), 0, VERSIONS), jax.random.fold_in(key_of[4], 1), 0, VERSIONS - 1).astype(jnp.int32)
    destination_keys = jax.random.split(jax.random.fold_in(key_of[5], 1), NT // TPS)
    destination_turns = jax.random.permutation(jax.random.fold_in(key_of[5], 3), NT // TPS)
    destination = jax.vmap(lambda own, number: routed_block(jax.random.fold_in(key_of[5], 2), own, number, TPS, N_LEARN, 1, CAP, 2))(destination_keys, destination_turns).reshape((NT, 1))
    w_key = noise(key_of[6], (D, KD), D ** -0.5, 0.078125)
    in_gain = jnp.clip(1.0 + 0.1 * jax.random.normal(key_of[7], (D,), jnp.float32), 0.5, 1.5)
    key_gain = jnp.clip(1.0 + 0.1 * jax.random.normal(key_of[8], (HD,), jnp.float32), 0.5, 1.5)
    return {"hidden": hidden, "cotangent": cotangent, "importance": importance, "block_len": block_len, "version": version, "destination": destination, "w_key": w_key, "in_gain": in_gain, "key_gain": key_gain}


epsilon = 1e-06
clip_ratio = 2.0
staleness = 0.5

def token_weights(importance, block_len, version):
    tile_count = block_len.shape[0]
    inside = (lax.broadcasted_iota(jnp.int32, (tile_count, TILE), 1) < block_len[:, None]).astype(jnp.float32)
    stale_age = (VERSIONS - 1 - version).astype(jnp.float32)
    decay_factor = jnp.power(jnp.float32(staleness), stale_age)
    return jnp.minimum(importance, clip_ratio) * (decay_factor[:, None] * inside).reshape(-1)

def layer_pass(hidden, upstream_rows, w_key, in_gain, key_gain):
    row_count = hidden.shape[0]
    x_float = hidden.astype(jnp.float32)
    inv_rms = lax.rsqrt(lax.optimization_barrier(jnp.mean(x_float * x_float, -1, keepdims=True)) + epsilon)
    normed = x_float * inv_rms
    h_rows = (normed * in_gain).astype(jnp.bfloat16)
    key_rows = jnp.dot(h_rows, w_key, preferred_element_type=jnp.float32).reshape(row_count, -1, key_gain.shape[0])
    key_scale = lax.rsqrt(lax.optimization_barrier(jnp.mean(key_rows * key_rows, -1, keepdims=True)) + epsilon)
    upstream = upstream_rows.astype(jnp.float32).reshape(key_rows.shape)
    kgain_part = lax.optimization_barrier(jnp.sum(upstream * key_rows * key_scale, axis=(0, 1)))
    scaled = upstream * key_gain
    grad_keys = key_scale * scaled - key_rows * key_scale ** 3 * lax.optimization_barrier(jnp.mean(scaled * key_rows, -1, keepdims=True))
    grad_keys = grad_keys.reshape(row_count, -1).astype(jnp.bfloat16)
    grad_h = lax.dot_general(grad_keys, w_key, (((1,), (1,)), ((), ())), preferred_element_type=jnp.float32)
    gain_part = lax.optimization_barrier(jnp.sum(grad_h * normed, 0))
    grad_normed = grad_h * in_gain
    grad_input = inv_rms * (grad_normed - normed * lax.optimization_barrier(jnp.mean(grad_normed * normed, -1, keepdims=True)))
    return (grad_input.astype(jnp.bfloat16), h_rows, grad_keys, gain_part, kgain_part)

def reference(hidden, cotangent, importance, block_len, version, destination, w_key, in_gain, key_gain):
    weights = token_weights(importance, block_len, version)
    upstream_all = (cotangent.astype(jnp.float32) * weights[:, None]).astype(jnp.bfloat16)
    device_count = N_GEN * N_LEARN
    per_device = TPS * TILE

    def scan_step(totals, block_pair):
        hidden_block, upstream_block = block_pair
        grad_input, h_rows, grad_keys, gain_part, kgain_part = layer_pass(hidden_block, upstream_block, w_key, in_gain, key_gain)
        weight_sum = totals[0] + lax.dot_general(h_rows, grad_keys, (((0,), (0,)), ((), ())), preferred_element_type=jnp.float32)
        return ((weight_sum, totals[1] + gain_part, totals[2] + kgain_part), grad_input)
    initial = (jnp.zeros((D, KD), jnp.float32), jnp.zeros((D,), jnp.float32), jnp.zeros((HD,), jnp.float32))
    totals, grad_blocks = lax.scan(scan_step, initial, (hidden.reshape(device_count, per_device, D), upstream_all.reshape(device_count, per_device, KD)))
    grad_tiles = grad_blocks.reshape(device_count * TPS, TILE, D)
    dest_device = destination[:, 0].reshape(device_count, TPS)
    onehot = (dest_device[:, :, None] == jnp.arange(N_LEARN, dtype=jnp.int32)[None, None, :]).astype(jnp.int32)
    slot_rank = lax.optimization_barrier(jnp.sum((jnp.cumsum(onehot, 1) - onehot) * onehot, -1))
    device_ids = jnp.arange(device_count, dtype=jnp.int32)[:, None]
    gen_ids = device_ids // N_LEARN
    learn_ids = device_ids % N_LEARN
    target = ((gen_ids * N_LEARN + dest_device) * SLOTS + learn_ids * CAP + slot_rank).reshape(-1)
    slots_out = jnp.zeros((device_count * SLOTS, TILE, D), jnp.bfloat16).at[target].set(grad_tiles)
    return (slots_out.reshape(-1, D), totals[0], totals[1], totals[2])
```

```python
import jax
import jax.numpy as jnp
from jax import lax
from jax.sharding import PartitionSpec as P

TILE = 8
VERSIONS = 4
SLOTS = 64


epsilon = 1e-06
clip_ratio = 2.0
staleness = 0.5


def token_weights(importance, block_len, version):
    tile_count = block_len.shape[0]
    inside = (lax.broadcasted_iota(jnp.int32, (tile_count, TILE), 1) < block_len[:, None]).astype(
        jnp.float32
    )
    stale_age = (VERSIONS - 1 - version).astype(jnp.float32)
    decay_factor = jnp.power(jnp.float32(staleness), stale_age)
    return jnp.minimum(importance, clip_ratio) * (decay_factor[:, None] * inside).reshape(-1)


def swap(x, axis, size, bit):
    return lax.ppermute(x, axis, [(i, i ^ bit) for i in range(size)])


def shift(x, axis, size, step):
    return lax.ppermute(x, axis, [(i, (i + step) % size) for i in range(size)])


def butterfly_sum(x, axes):
    for axis, size in axes:
        bit = 1
        while bit < size:
            x = x + swap(x, axis, size, bit)
            bit *= 2
    return x


def join(mine, other, upper):
    place = lax.broadcasted_iota(jnp.int32, (2,) + (1,) * mine.ndim, 0)
    both = jnp.where(place == upper, mine[None], other[None])
    return both.reshape((2 * mine.shape[0],) + mine.shape[1:])


def dot_rows(a, b):
    return lax.dot_general(a, b, (((0,), (0,)), ((), ())), preferred_element_type=jnp.float32)


def weight_gradient(h_rows, grad_keys, gens, learners):
    gen, learn = lax.axis_index("gen"), lax.axis_index("learn")
    width = h_rows.shape[1] // gens
    half = width // 2

    def columns(step):
        return lax.dynamic_slice_in_dim(h_rows, ((gen + step) % gens) * width, width, 1)

    h_all, k_all = [columns(0)], [grad_keys]
    for step in range(1, gens):
        h_all.append(shift(columns(step), "gen", gens, step))
        k_all.append(shift(grad_keys, "gen", gens, step))
    core = learn % 2
    total = 0.0
    for h_part, k_part in zip(h_all, k_all):
        own = lax.dynamic_slice_in_dim(h_part, core * half, half, 1)
        for_other = lax.dynamic_slice_in_dim(h_part, (1 - core) * half, half, 1)
        total = total + dot_rows(own, k_part)
        total = total + dot_rows(
            swap(for_other, "learn", learners, 1), swap(k_part, "learn", learners, 1)
        )
    bits = []
    bit = 2
    while bit < learners:
        upper = (learn // bit) % 2
        rows = total.shape[0] // 2
        sent = lax.dynamic_slice_in_dim(total, (1 - upper) * rows, rows, 0).astype(jnp.bfloat16)
        kept = lax.dynamic_slice_in_dim(total, upper * rows, rows, 0)
        total = kept + swap(sent, "learn", learners, bit).astype(jnp.float32)
        bits.append(bit)
        bit *= 2
    block = total.astype(jnp.bfloat16)
    for bit in reversed(bits):
        block = join(block, swap(block, "learn", learners, bit), (learn // bit) % 2)
    other = swap(block, "learn", learners, 1)
    return join(block.astype(jnp.float32), other.astype(jnp.float32), core)


def body(hidden, cotangent, importance, block_len, version, destination, w_key, in_gain, key_gain):
    learners = lax.axis_size("learn")
    gens = lax.axis_size("gen")
    capacity = SLOTS // learners
    tile_count = block_len.shape[0]
    row_count = hidden.shape[0]
    weights = token_weights(importance, block_len, version)
    upstream_all = (cotangent.astype(jnp.float32) * weights[:, None]).astype(jnp.bfloat16)
    dest_column = destination[:, 0]
    onehot = (dest_column[:, None] == jnp.arange(learners, dtype=jnp.int32)[None, :]).astype(
        jnp.int32
    )
    slot_rank = jnp.sum((jnp.cumsum(onehot, 0) - onehot) * onehot, 1)
    target = dest_column * capacity + slot_rank
    rows_to = (target[:, None] * TILE + jnp.arange(TILE, dtype=jnp.int32)[None, :]).reshape(-1)
    placing = (
        rows_to[None, :] == jnp.arange(SLOTS * TILE, dtype=jnp.int32)[:, None]
    ).astype(jnp.bfloat16)

    x_float = hidden.astype(jnp.float32)
    inv_rms = lax.rsqrt(jnp.mean(x_float * x_float, -1, keepdims=True) + epsilon)
    normed = x_float * inv_rms
    h_rows = (normed * in_gain).astype(jnp.bfloat16)
    key_rows = jnp.dot(h_rows, w_key, preferred_element_type=jnp.float32).reshape(
        row_count, -1, key_gain.shape[0]
    )
    key_scale = lax.rsqrt(jnp.mean(key_rows * key_rows, -1, keepdims=True) + epsilon)
    upstream = upstream_all.astype(jnp.float32).reshape(key_rows.shape)
    kgain_part = jnp.sum(upstream * key_rows * key_scale, axis=(0, 1))
    scaled = upstream * key_gain
    grad_keys = key_scale * scaled - key_rows * key_scale**3 * jnp.mean(
        scaled * key_rows, -1, keepdims=True
    )
    grad_keys = grad_keys.reshape(row_count, -1).astype(jnp.bfloat16)
    grad_h = lax.dot_general(
        grad_keys, w_key, (((1,), (1,)), ((), ())), preferred_element_type=jnp.float32
    )
    gain_part = jnp.sum(grad_h * normed, 0)
    grad_normed = grad_h * in_gain
    grad_input = inv_rms * (
        grad_normed - normed * jnp.mean(grad_normed * normed, -1, keepdims=True)
    )
    spread = jnp.dot(
        placing, grad_input.astype(jnp.bfloat16), preferred_element_type=jnp.float32
    ).astype(jnp.bfloat16)
    grad_slots = lax.all_to_all(spread, "learn", split_axis=0, concat_axis=0, tiled=True)
    w_grad = weight_gradient(h_rows, grad_keys, gens, learners)
    features = hidden.shape[1]
    sums = butterfly_sum(
        jnp.concatenate([gain_part, kgain_part]), (("gen", gens), ("learn", learners))
    )
    return (grad_slots, w_grad, sums[:features], sums[features:])


def solution(mesh):
    return jax.shard_map(
        body,
        mesh=mesh,
        in_specs=(
            P(("gen", "learn"), None),
            P(("gen", "learn"), None),
            P(("gen", "learn")),
            P(("gen", "learn")),
            P(("gen", "learn")),
            P(("gen", "learn"), None),
            P(),
            P(),
            P(),
        ),
        out_specs=(P(("gen", "learn"), None), P("gen", None), P(), P()),
        check_vma=False,
    )
```

```python
import jax
import jax.numpy as jnp
from jax import lax
from jax.sharding import PartitionSpec as P

TILE = 8
VERSIONS = 4
SLOTS = 64
PACKET = 72
PASSED_ON = 48
TAGS = 128


epsilon = 1e-06
clip_ratio = 2.0
staleness = 0.5


def token_weights(importance, block_len, version):
    tile_count = block_len.shape[0]
    inside = (lax.broadcasted_iota(jnp.int32, (tile_count, TILE), 1) < block_len[:, None]).astype(
        jnp.float32
    )
    stale_age = (VERSIONS - 1 - version).astype(jnp.float32)
    decay_factor = jnp.power(jnp.float32(staleness), stale_age)
    return jnp.minimum(importance, clip_ratio) * (decay_factor[:, None] * inside).reshape(-1)


def swap(x, axis, size, bit):
    return lax.ppermute(x, axis, [(i, i ^ bit) for i in range(size)])


def shift(x, axis, size, step):
    return lax.ppermute(x, axis, [(i, (i + step) % size) for i in range(size)])


def butterfly_sum(x, axes):
    for axis, size in axes:
        bit = 1
        while bit < size:
            x = x + swap(x, axis, size, bit)
            bit *= 2
    return x


def join(mine, other, upper):
    place = lax.broadcasted_iota(jnp.int32, (2,) + (1,) * mine.ndim, 0)
    both = jnp.where(place == upper, mine[None], other[None])
    return both.reshape((2 * mine.shape[0],) + mine.shape[1:])


def dot_rows(a, b):
    return lax.dot_general(a, b, (((0,), (0,)), ((), ())), preferred_element_type=jnp.float32)


def weight_gradient(h_rows, grad_keys, gens, learners):
    gen, learn = lax.axis_index("gen"), lax.axis_index("learn")
    width = h_rows.shape[1] // gens
    half = width // 2

    def columns(step):
        return lax.dynamic_slice_in_dim(h_rows, ((gen + step) % gens) * width, width, 1)

    h_all, k_all = [columns(0)], [grad_keys]
    for step in range(1, gens):
        h_all.append(shift(columns(step), "gen", gens, step))
        k_all.append(shift(grad_keys, "gen", gens, step))
    core = learn % 2
    total = 0.0
    for h_part, k_part in zip(h_all, k_all):
        own = lax.dynamic_slice_in_dim(h_part, core * half, half, 1)
        for_other = lax.dynamic_slice_in_dim(h_part, (1 - core) * half, half, 1)
        total = total + dot_rows(own, k_part)
        total = total + dot_rows(
            swap(for_other, "learn", learners, 1), swap(k_part, "learn", learners, 1)
        )
    bits = []
    bit = 2
    while bit < learners:
        upper = (learn // bit) % 2
        rows = total.shape[0] // 2
        sent = lax.dynamic_slice_in_dim(total, (1 - upper) * rows, rows, 0).astype(jnp.bfloat16)
        kept = lax.dynamic_slice_in_dim(total, upper * rows, rows, 0)
        total = kept + swap(sent, "learn", learners, bit).astype(jnp.float32)
        bits.append(bit)
        bit *= 2
    block = total.astype(jnp.bfloat16)
    for bit in reversed(bits):
        block = join(block, swap(block, "learn", learners, bit), (learn // bit) % 2)
    other = swap(block, "learn", learners, 1)
    return join(block.astype(jnp.float32), other.astype(jnp.float32), core)


def swap_dense(grad_input, target, learners):
    rows_to = (target[:, None] * TILE + jnp.arange(TILE, dtype=jnp.int32)[None, :]).reshape(-1)
    place = jnp.arange(SLOTS * TILE, dtype=jnp.int32)[:, None]
    spread = jnp.dot(
        (rows_to[None, :] == place).astype(jnp.bfloat16),
        grad_input,
        preferred_element_type=jnp.float32,
    )
    return lax.all_to_all(
        spread.astype(jnp.bfloat16), "learn", split_axis=0, concat_axis=0, tiled=True
    )


def packet_plan(block_len, dest_column, slot_rank, learners):
    learn = lax.axis_index("learn")
    planes = learners // 4
    capacity = SLOTS // learners
    packet = min(PACKET, 4 * capacity * TILE)
    passed_on = min(PASSED_ON, 2 * capacity * TILE)
    rows = block_len.shape[0] * TILE
    row = jnp.arange(rows, dtype=jnp.int32)
    dest = jnp.repeat(dest_column, TILE)
    valid = row % TILE < jnp.repeat(block_len, TILE)
    apart = dest ^ learn
    plane = jnp.where(valid, apart // 4, planes)
    other_y = (apart // 2) % 2
    kinds = jnp.arange(2 * planes, dtype=jnp.int32)
    member = (plane * 2 + other_y)[None, :] == kinds[:, None]
    before = (row[:, None] < row[None, :]).astype(jnp.bfloat16)
    ahead = jnp.dot(
        member.astype(jnp.bfloat16), before, preferred_element_type=jnp.float32
    ).astype(jnp.int32)
    count = jnp.sum(member.astype(jnp.int32), 1)
    start = (kinds // 2) * packet + jnp.where(kinds % 2 == 1, packet - count, 0)
    position = jnp.sum(jnp.where(member, ahead + start[:, None], 0), 0)
    position = jnp.where(valid, position, -1)
    count = count.reshape(planes, 2)
    over = jnp.any((count[:, 0] + count[:, 1] > packet) | (count[:, 1] > passed_on))
    slot = learn * capacity + jnp.repeat(slot_rank, TILE)
    tags = jnp.stack([dest + 1, slot, row % TILE], 1)
    tags = jnp.pad(tags, ((0, 0), (0, TAGS - 3))).astype(jnp.bfloat16)
    return position, tags, over, packet, passed_on


def swap_packets(rows_with_tags, position, packet, passed_on, learners):
    planes = learners // 4
    place = jnp.arange(planes * packet, dtype=jnp.int32)[:, None]
    packed = jnp.dot(
        (position[None, :] == place).astype(jnp.bfloat16),
        rows_with_tags,
        preferred_element_type=jnp.float32,
    ).astype(jnp.bfloat16)
    held = []
    for k in range(planes):
        part = packed[k * packet : (k + 1) * packet]
        if k:
            part = swap(part, "learn", learners, 4 * k)
        held.append(part)
    held += [swap(part[packet - passed_on :], "learn", learners, 2) for part in held]
    held += [swap(part, "learn", learners, 1) for part in held]
    return held


def place_packets(held, features):
    everything = jnp.concatenate(held, 0)
    tags = everything[:, features : features + 3].astype(jnp.int32)
    mine = tags[:, 0] == lax.axis_index("learn") + 1
    target = jnp.where(mine, tags[:, 1] * TILE + tags[:, 2], -1)
    place = jnp.arange(SLOTS * TILE, dtype=jnp.int32)[None, :]
    return dot_rows(
        (target[:, None] == place).astype(jnp.bfloat16), everything[:, :features]
    ).astype(jnp.bfloat16)


def body(hidden, cotangent, importance, block_len, version, destination, w_key, in_gain, key_gain):
    learners = lax.axis_size("learn")
    gens = lax.axis_size("gen")
    capacity = SLOTS // learners
    tile_count = block_len.shape[0]
    row_count = hidden.shape[0]
    weights = token_weights(importance, block_len, version)
    upstream_all = (cotangent.astype(jnp.float32) * weights[:, None]).astype(jnp.bfloat16)
    dest_column = destination[:, 0]
    onehot = (dest_column[:, None] == jnp.arange(learners, dtype=jnp.int32)[None, :]).astype(
        jnp.int32
    )
    slot_rank = jnp.sum((jnp.cumsum(onehot, 0) - onehot) * onehot, 1)
    target = dest_column * capacity + slot_rank
    position, tags, over, packet, passed_on = packet_plan(
        block_len, dest_column, slot_rank, learners
    )

    x_float = hidden.astype(jnp.float32)
    inv_rms = lax.rsqrt(jnp.mean(x_float * x_float, -1, keepdims=True) + epsilon)
    normed = x_float * inv_rms
    h_rows = (normed * in_gain).astype(jnp.bfloat16)
    key_rows = jnp.dot(h_rows, w_key, preferred_element_type=jnp.float32).reshape(
        row_count, -1, key_gain.shape[0]
    )
    key_scale = lax.rsqrt(jnp.mean(key_rows * key_rows, -1, keepdims=True) + epsilon)
    upstream = upstream_all.astype(jnp.float32).reshape(key_rows.shape)
    kgain_part = jnp.sum(upstream * key_rows * key_scale, axis=(0, 1))
    scaled = upstream * key_gain
    grad_keys = key_scale * scaled - key_rows * key_scale**3 * jnp.mean(
        scaled * key_rows, -1, keepdims=True
    )
    grad_keys = grad_keys.reshape(row_count, -1).astype(jnp.bfloat16)
    grad_h = lax.dot_general(
        grad_keys, w_key, (((1,), (1,)), ((), ())), preferred_element_type=jnp.float32
    )
    gain_part = jnp.sum(grad_h * normed, 0)
    grad_normed = grad_h * in_gain
    grad_input = inv_rms * (
        grad_normed - normed * jnp.mean(grad_normed * normed, -1, keepdims=True)
    )
    grad_input = grad_input.astype(jnp.bfloat16)
    held = swap_packets(
        jnp.concatenate([grad_input, tags], 1), position, packet, passed_on, learners
    )
    w_grad = weight_gradient(h_rows, grad_keys, gens, learners)
    features = hidden.shape[1]
    flag = jnp.where(over, 1.0, 0.0) * jnp.ones((key_gain.shape[0],), jnp.float32)
    sums = butterfly_sum(
        jnp.concatenate([gain_part, kgain_part, flag]), (("gen", gens), ("learn", learners))
    )
    grad_slots = lax.cond(
        sums[-1] > 0.5,
        lambda: swap_dense(grad_input, target, learners),
        lambda: place_packets(held, features),
    )
    heads_end = features + key_gain.shape[0]
    return (grad_slots, w_grad, sums[:features], sums[features:heads_end])


def solution(mesh):
    return jax.shard_map(
        body,
        mesh=mesh,
        in_specs=(
            P(("gen", "learn"), None),
            P(("gen", "learn"), None),
            P(("gen", "learn")),
            P(("gen", "learn")),
            P(("gen", "learn")),
            P(("gen", "learn"), None),
            P(),
            P(),
            P(),
        ),
        out_specs=(P(("gen", "learn"), None), P("gen", None), P(), P()),
        check_vma=False,
    )
```

```python
import functools

import jax
import jax.numpy as jnp
from jax import lax
from jax.experimental import pallas as pl
from jax.experimental.pallas import tpu as pltpu
from jax.sharding import PartitionSpec as P

TILE = 8
VERSIONS = 4
SLOTS = 64
PACKET = 72
PASSED_ON = 48
TAGS = 128
STRIP = 512
UNROLL = 5
KEYS_MIB, STACK_MIB, PLACE_MIB, SLOTS_MIB = 36, 20, 30, 44


epsilon = 1e-06
clip_ratio = 2.0
staleness = 0.5
BOTH = ("gen", "learn")
F32 = jnp.float32
BF16 = jnp.bfloat16


def to_column(row, size):
    same = lax.broadcasted_iota(jnp.int32, (size, size), 0) == lax.broadcasted_iota(
        jnp.int32, (size, size), 1
    )
    return jnp.sum(jnp.where(same, row, jnp.zeros_like(row)), 1, keepdims=True)


def row_values(per_block, rows):
    shape = (rows, per_block.shape[1])
    own = lax.broadcasted_iota(jnp.int32, shape, 0) // TILE == lax.broadcasted_iota(
        jnp.int32, shape, 1
    )
    return jnp.sum(jnp.where(own, per_block, jnp.zeros_like(per_block)), 1, keepdims=True)


def token_weights(importance_row, len_row, version_row):
    rows = importance_row.shape[1]
    stale_age = VERSIONS - 1 - version_row
    decay_row = jnp.zeros(stale_age.shape, F32)
    for age in range(VERSIONS):
        decay_row = jnp.where(stale_age == age, staleness**age, decay_row)
    inside = lax.broadcasted_iota(jnp.int32, (rows, 1), 0) % TILE < row_values(len_row, rows)
    importance = jnp.minimum(to_column(importance_row, rows), clip_ratio)
    return importance * (row_values(decay_row, rows) * jnp.where(inside, 1.0, 0.0))


def swap(x, axis, size, bit):
    return lax.ppermute(x, axis, [(i, i ^ bit) for i in range(size)])


def butterfly_sum(x, axes, learners=None):
    for axis, size in axes:
        bit = 1
        while bit < size:
            x = x + swap(x, axis, learners or size, bit)
            bit *= 2
    return x


def join_at(mine, other, upper, axis):
    place = lax.broadcasted_iota(jnp.int32, (2,) + (1,) * (mine.ndim - axis), 0)
    return jnp.where(
        place == upper, jnp.expand_dims(mine, axis), jnp.expand_dims(other, axis)
    )


def join(mine, other, upper):
    return join_at(mine, other, upper, 0).reshape((2 * mine.shape[0],) + mine.shape[1:])


def dot_rows(a, b):
    return lax.dot_general(a, b, (((0,), (0,)), ((), ())), preferred_element_type=F32)


VMEM = pl.BlockSpec(memory_space=pltpu.VMEM)
SMEM = pl.BlockSpec(memory_space=pltpu.SMEM)
ANY = pl.BlockSpec(memory_space=pl.ANY)


def keys_kernel(blocks, plan, pieces, index_ref, *refs):
    sources, outs, refs = refs[:9], refs[9 : 9 + blocks], refs[9 + blocks :]
    planes, packet = plan[:2]
    packs, refs = refs[: len(pieces)], refs[len(pieces) :]
    (keys_out, sums_out), held, (w_all, h_all, keys, sems) = refs[:2], refs[2:10], refs[10:]

    def spread(packed, first):
        for pack, (low, high) in zip(packs, pieces):
            pack[:, first] = packed[low:high]

    w_ref = sources[8]
    copies = [
        pltpu.make_async_copy(source, place, sems.at[i])
        for i, (source, place) in enumerate(zip(sources[:8], held))
    ]
    for copy in copies:
        copy.start()
    hidden_ref, len_ref, dest_ref, importance_ref, version_ref, gain_ref, key_gain_ref = held[:7]
    cotangent_ref = held[7]
    rows, features = hidden_ref.shape
    strips = features // STRIP

    def strip(i):
        return pl.ds(pl.multiple_of(i * STRIP, STRIP), STRIP)

    def fetch(i):
        return pltpu.make_async_copy(w_ref.at[strip(i)], w_all.at[strip(i)], sems.at[8 + i])

    for i in range(strips):
        fetch(i).start()
    for copy in copies[1:3]:
        copy.wait()
    place, tags, over = packet_plan(index_ref[blocks], len_ref[...], dest_ref[...], rows, *plan)
    places = lax.broadcasted_iota(jnp.int32, (planes * packet, rows), 0)
    onehot = (places == place).astype(F32).astype(BF16)
    for copy in copies[3:]:
        copy.wait()
    weight = token_weights(importance_ref[...], len_ref[...], version_ref[...])
    copies[0].wait()

    def squares(i, total):
        part = hidden_ref[:, strip(i)]
        packed = jnp.dot(onehot, part, preferred_element_type=F32).astype(BF16)
        spread(packed, strip(i))
        x = part.astype(F32)
        return total + jnp.sum(x * x, 1, keepdims=True)

    square_sum = lax.fori_loop(
        0, strips, squares, jnp.zeros((rows, 1), F32), unroll=UNROLL
    )
    packed = jnp.dot(onehot, tags, preferred_element_type=F32).astype(BF16)
    spread(packed, slice(features, features + TAGS))
    inv = lax.rsqrt(square_sum / features + epsilon)
    keys[...] = jnp.zeros_like(keys)

    def project(i, carry):
        h = (hidden_ref[:, strip(i)].astype(F32) * inv * gain_ref[:, strip(i)]).astype(BF16)
        h_all[:, strip(i)] = h
        fetch(i).wait()
        keys[...] += jnp.dot(h, w_all[strip(i), :], preferred_element_type=F32)
        return carry

    lax.fori_loop(0, strips, project, 0, unroll=UNROLL)
    width = outs[0].shape[1] - keys.shape[1]
    for k in range(blocks):
        outs[k][:, :width] = h_all[:, pl.ds(pl.multiple_of(index_ref[k] * width, width), width)]
    head = key_gain_ref.shape[1]
    kgain = jnp.zeros((1, head), F32)
    for a in range(keys.shape[1] // head):
        span = slice(a * head, (a + 1) * head)
        key = keys[:, span]
        scale = lax.rsqrt(jnp.mean(key * key, 1, keepdims=True) + epsilon)
        upstream = (cotangent_ref[:, span].astype(F32) * weight).astype(BF16).astype(F32)
        kgain = kgain + jnp.sum(upstream * key * scale, 0, keepdims=True)
        scaled = upstream * key_gain_ref[...]
        grad = scale * scaled - key * (scale * scale * scale) * jnp.mean(
            scaled * key, 1, keepdims=True
        )
        grad = grad.astype(BF16)
        keys_out[:, span] = grad
        for k in range(blocks):
            outs[k][:, width + a * head : width + (a + 1) * head] = grad
    sums_out[:, :head] = kgain
    sums_out[:, head:] = jnp.broadcast_to(over, (1, head))
    packed = jnp.dot(onehot, keys_out[...], preferred_element_type=F32).astype(BF16)
    spread(packed, slice(features + TAGS, features + TAGS + keys.shape[1]))


def packet_plan(learn, len_row, dest_row, rows, planes, packet, passed_on, capacity):
    tiles = dest_row.shape[1]
    dest_column = to_column(dest_row, tiles)
    shape = (tiles, tiles)
    earlier = lax.broadcasted_iota(jnp.int32, shape, 0) < lax.broadcasted_iota(jnp.int32, shape, 1)
    alike = earlier & (dest_column == dest_row)
    rank_row = jnp.sum(jnp.where(alike, 1, 0), 0, keepdims=True)
    shape = (tiles, rows)
    token = lax.broadcasted_iota(jnp.int32, shape, 1)
    own = token // TILE == lax.broadcasted_iota(jnp.int32, shape, 0)
    dest = jnp.sum(jnp.where(own, dest_column, 0), 0, keepdims=True)
    length = jnp.sum(jnp.where(own, to_column(len_row, tiles), 0), 0, keepdims=True)
    valid = token[:1] % TILE < length
    apart = dest ^ learn
    kind = jnp.where(valid, (apart // 4) * 2 + (apart // 2) % 2, 2 * planes)
    kinds = lax.broadcasted_iota(jnp.int32, (2 * planes, 1), 0)
    member = kind == kinds
    shape = (rows, rows)
    before = lax.broadcasted_iota(jnp.int32, shape, 0) < lax.broadcasted_iota(jnp.int32, shape, 1)
    counted = jnp.where(member, 1.0, 0.0)
    ahead = jnp.dot(
        counted.astype(BF16),
        jnp.where(before, 1.0, 0.0).astype(BF16),
        preferred_element_type=F32,
    ).astype(jnp.int32)
    count = jnp.sum(counted, 1, keepdims=True).astype(jnp.int32)
    start = (kinds // 2) * packet + jnp.where(kinds % 2 == 1, packet - count, 0)
    position = jnp.sum(jnp.where(member, ahead + start, 0), 0, keepdims=True)
    position = jnp.where(valid, position, -1)
    plane_of = lax.broadcasted_iota(jnp.int32, (2 * planes, planes), 0) // 2
    same_plane = plane_of == lax.broadcasted_iota(jnp.int32, (2 * planes, planes), 1)
    together = jnp.sum(jnp.where(same_plane, count, 0), 0, keepdims=True)
    too_many = jnp.where((kinds % 2 == 1) & (count > passed_on), 1.0, 0.0)
    over = jnp.max(jnp.where(together > packet, 1.0, 0.0), 1, keepdims=True) + jnp.max(
        too_many, 0, keepdims=True
    )
    lane = lax.broadcasted_iota(jnp.int32, (rows, TAGS), 1)
    line = lax.broadcasted_iota(jnp.int32, (rows, TAGS), 0) % TILE
    slot = learn * capacity + row_values(rank_row, rows)
    tags = jnp.where(lane == 0, row_values(dest_row, rows) + 1, jnp.where(lane == 1, slot, line))
    tags = jnp.where(lane < 3, tags, 0)
    return position, tags.astype(F32).astype(BF16), over


def stack_kernel(*refs):
    out, used = refs[-1], 0
    for part in refs[:-1]:
        out[used : used + part.shape[0], :] = part[...]
        used += part.shape[0]
    if used < out.shape[0]:
        out[used:, :] = jnp.zeros((out.shape[0] - used, out.shape[1]), BF16)


def place_kernel(me_ref, own_ref, other_ref, rows_out, keys_out, chosen):
    slots, features = rows_out.shape
    count = own_ref.shape[0]
    tag = slice(features, features + TAGS)
    tags = jnp.concatenate([own_ref[:, tag], other_ref[:, tag]], 0)
    tags = tags.astype(F32).T.astype(jnp.int32)
    target = jnp.where(tags[0:1] == me_ref[0] + 1, tags[1:2] * TILE + tags[2:3], -1)
    places = lax.broadcasted_iota(jnp.int32, (slots, 2 * count), 0)
    chosen[...] = (places == target).astype(F32).astype(BF16)

    def pick(columns):
        rows = jnp.dot(chosen[:, :count], own_ref[:, columns], preferred_element_type=F32)
        rows += jnp.dot(chosen[:, count:], other_ref[:, columns], preferred_element_type=F32)
        return rows.astype(BF16)

    def put(i, carry):
        strip = pl.ds(pl.multiple_of(i * STRIP, STRIP), STRIP)
        rows_out[:, strip] = pick(strip)
        return carry

    lax.fori_loop(0, features // STRIP, put, 0, unroll=UNROLL)
    keys_out[...] = pick(slice(features + TAGS, features + TAGS + keys_out.shape[1]))


def slots_kernel(over_ref, rows_ref, keys_ref, w_ref, gain_ref, out_ref, w_all, grad, sems):
    slots, features = out_ref.shape
    strips = features // STRIP

    def strip(i):
        return pl.ds(pl.multiple_of(i * STRIP, STRIP), STRIP)

    def fetch(i):
        return pltpu.make_async_copy(w_ref.at[strip(i)], w_all.at[strip(i)], sems.at[i])

    for i in range(strips):
        fetch(i).start()

    def back(i, total):
        rows = rows_ref[:, strip(i)].astype(F32)
        fetch(i).wait()
        g = gain_ref[:, strip(i)] * lax.dot_general(
            keys_ref[...], w_all[strip(i), :], (((1,), (1,)), ((), ())), preferred_element_type=F32
        )
        grad[:, strip(i)] = g
        squares, products = total
        return (
            squares + jnp.sum(rows * rows, 1, keepdims=True),
            products + jnp.sum(g * rows, 1, keepdims=True),
        )

    zero = jnp.zeros((slots, 1), F32)
    squares, products = lax.fori_loop(0, strips, back, (zero, zero), unroll=UNROLL)
    inv = lax.rsqrt(squares / features + epsilon)
    mean = products * inv / features

    def finish(i, carry):
        normed = rows_ref[:, strip(i)].astype(F32) * inv
        out_ref[:, strip(i)] = (inv * (grad[:, strip(i)] - normed * mean)).astype(BF16)
        return carry

    lax.fori_loop(0, strips, finish, 0, unroll=UNROLL)

    @pl.when(over_ref[0] > 0.5)
    def _():
        out_ref[...] = rows_ref[...]


def output_kernel(sizes, index_ref, *refs):
    count = len(sizes)
    mine, others, out_ref = refs[:count], refs[count : 2 * count], refs[-1]
    half = mine[0].shape[1]
    step = pl.program_id(0)
    core = index_ref[sum(sizes)]
    columns = pl.ds(pl.multiple_of(core * half, half), half)
    other_columns = pl.ds(pl.multiple_of((1 - core) * half, half), half)
    first = 0
    for k, size in enumerate(sizes):

        @pl.when((step >= first) & (step < first + size))
        def _():
            out_ref[:, columns] = mine[k][...].astype(F32)
            out_ref[:, other_columns] = others[k][...].astype(F32)

        first += size


def lay_out(index, mine, others, tall, rows, filled=None):
    half = mine[0].shape[1]
    sizes = [part.shape[0] // tall for part in mine]

    def spec(k):
        first, size = sum(sizes[:k]), sizes[k]
        return pl.BlockSpec((tall, half), lambda i, ids: (jnp.clip(i - first, 0, size - 1), 0))

    specs = [spec(k) for k in range(len(sizes))]
    more = [] if filled is None else [filled]
    return pl.pallas_call(
        functools.partial(output_kernel, sizes),
        out_shape=jax.ShapeDtypeStruct((rows, 2 * half), F32),
        grid_spec=pltpu.PrefetchScalarGridSpec(
            num_scalar_prefetch=1,
            grid=(sum(sizes),),
            in_specs=specs + specs + [ANY] * len(more),
            out_specs=pl.BlockSpec((tall, 2 * half), lambda i, ids: (ids[i], 0)),
        ),
        input_output_aliases={1 + 2 * len(sizes): 0} if more else {},
        compiler_params=pltpu.CompilerParams(vmem_limit_bytes=24 << 20),
    )(index, *mine, *others, *more)


def swap_dense(hidden, grad_keys, w_key, in_gain, dest_column, learners):
    x_float = hidden.astype(F32)
    inv_rms = lax.rsqrt(jnp.mean(x_float * x_float, -1, keepdims=True) + epsilon)
    normed = x_float * inv_rms
    grad_normed = in_gain * lax.dot_general(
        grad_keys, w_key, (((1,), (1,)), ((), ())), preferred_element_type=F32
    )
    grad_input = inv_rms * (
        grad_normed - normed * jnp.mean(grad_normed * normed, -1, keepdims=True)
    )
    onehot = (dest_column[:, None] == jnp.arange(learners, dtype=jnp.int32)[None, :]).astype(
        jnp.int32
    )
    slot_rank = jnp.sum((jnp.cumsum(onehot, 0) - onehot) * onehot, 1)
    target = dest_column * (SLOTS // learners) + slot_rank
    rows_to = (target[:, None] * TILE + jnp.arange(TILE, dtype=jnp.int32)[None, :]).reshape(-1)
    place = jnp.arange(SLOTS * TILE, dtype=jnp.int32)[:, None]
    spread = jnp.dot(
        (rows_to[None, :] == place).astype(BF16),
        grad_input.astype(BF16),
        preferred_element_type=F32,
    )
    return lax.all_to_all(spread.astype(BF16), "learn", split_axis=0, concat_axis=0, tiled=True)


def body(hidden, cotangent, importance, block_len, version, destination, w_key, in_gain, key_gain):
    learners, gens = lax.axis_size("learn"), lax.axis_size("gen")
    gen, learn = lax.axis_index("gen"), lax.axis_index("learn")
    core, across = learn % 2, (learn // 2) % 2
    capacity = SLOTS // learners
    planes = learners // 4
    packet = min(PACKET, 4 * capacity * TILE)
    passed_on = min(PASSED_ON, 2 * capacity * TILE)
    rows, features = hidden.shape
    key_count = cotangent.shape[1]
    head = key_gain.shape[0]
    strips = features // STRIP
    blocks = 2 * gens
    width = features // blocks
    half = key_count // 2

    def limit(mebibytes):
        return pltpu.CompilerParams(vmem_limit_bytes=mebibytes << 20)


    front = packet - passed_on
    pieces = []
    for k in range(planes):
        cuts = (0, front, packet) if k in (0, planes - 1) else (0, packet)
        pieces += [(k * packet + low, k * packet + high) for low, high in zip(cuts, cuts[1:])]
    packed_width = features + TAGS + key_count
    steps = [(step, dy) for step in range(gens) for dy in range(2)]
    wanted = [((gen + step) % gens) * 2 + (across ^ dy) for step, dy in steps]
    in_gain_row = in_gain[None, :]
    tiles = block_len.shape[0]
    made = pl.pallas_call(
        functools.partial(
            keys_kernel, blocks, (planes, packet, passed_on, capacity), pieces
        ),
        out_shape=[jax.ShapeDtypeStruct((rows, width + key_count), BF16)] * blocks
        + [jax.ShapeDtypeStruct((high - low, packed_width), BF16) for low, high in pieces]
        + [
            jax.ShapeDtypeStruct((rows, key_count), BF16),
            jax.ShapeDtypeStruct((1, 2 * head), F32),
        ],
        in_specs=[SMEM] + [ANY] * 9,
        out_specs=[VMEM] * (blocks + len(pieces) + 2),
        scratch_shapes=[
            pltpu.VMEM((rows, features), BF16),
            pltpu.VMEM((1, tiles), jnp.int32),
            pltpu.VMEM((1, tiles), jnp.int32),
            pltpu.VMEM((1, rows), F32),
            pltpu.VMEM((1, tiles), jnp.int32),
            pltpu.VMEM((1, features), F32),
            pltpu.VMEM((1, head), F32),
            pltpu.VMEM((rows, key_count), BF16),
            pltpu.VMEM((features, key_count), BF16),
            pltpu.VMEM((rows, features), BF16),
            pltpu.VMEM((rows, key_count), F32),
            pltpu.SemaphoreType.DMA((8 + strips,)),
        ],
        compiler_params=limit(KEYS_MIB),
        cost_estimate=pl.CostEstimate(
            flops=2 * rows * features * key_count, bytes_accessed=16 << 20, transcendentals=0
        ),
    )(
        jnp.stack(wanted + [learn]),
        hidden,
        block_len[None, :],
        destination[:, 0][None, :],
        importance[None, :],
        version[None, :],
        in_gain_row,
        key_gain[None, :],
        cotangent,
        w_key,
    )
    operands, packs, (grad_keys, sums) = (
        made[:blocks],
        made[blocks : blocks + len(pieces)],
        made[blocks + len(pieces) :],
    )

    def gather(k):
        step, dy = steps[k]
        pairs = [
            (p * learners + j, ((p + step) % gens) * learners + (j ^ (2 * dy)))
            for p in range(gens)
            for j in range(learners)
        ]
        return lax.ppermute(operands[k], BOTH, pairs)

    def across_learn(part, bit):
        return swap(part, "learn", learners, bit)

    def over_y(part):
        return across_learn(part[part.shape[0] - passed_on :], 2)

    def products(part):
        keys = lax.dynamic_slice_in_dim(part, width + core * half, half, 1)
        return dot_rows(part[:, :width], keys)

    barrier = lax.optimization_barrier
    direct = [k for k, (step, dy) in enumerate(steps) if (step > 0) + dy == 1]
    diagonal = [k for k, (step, dy) in enumerate(steps) if (step > 0) + dy == 2]
    last = planes - 1
    held, passed = {0: packs[1], planes: packs[0]}, {}

    gathered = [gather(k) for k in direct + diagonal]
    for k in range(2, last):
        held[k] = across_learn(packs[1 + k], 4 * k)
    held[planes + 1] = across_learn(packs[-2], 4 * last)
    gathered, held, packs = barrier((gathered, held, packs))

    total = products(operands[0]) + products(across_learn(operands[0], 1))
    for part in gathered:
        total = total + products(part) + products(across_learn(part, 1))
    held[1] = across_learn(packs[2], 4)
    held[last] = across_learn(packs[-1], 4 * last)
    for k in (0, *range(2, last)):
        passed[k] = over_y(held[k])
    total, held, passed = barrier((total, held, passed))

    bits = [4 << b for b in range(planes.bit_length() - 1)]
    for n, bit in enumerate(bits):
        upper = (learn // bit) % 2
        tall = total.shape[0] // 2
        sent = lax.dynamic_slice_in_dim(total, (1 - upper) * tall, tall, 0).astype(BF16)
        kept = lax.dynamic_slice_in_dim(total, upper * tall, tall, 0)
        total = kept + across_learn(sent, bit).astype(F32)
        if n == 0:
            passed[1] = over_y(held[1])
            sums = butterfly_sum(sums, (("gen", gens),))
            sums = butterfly_sum(sums, (("learn", 4),), learners)
        if n == 1:
            passed[last] = over_y(held[last])
            sums = sums + across_learn(sums, bits[0])
        total, passed, held, sums = barrier((total, passed, held, sums))

    tall = total.shape[0]
    first = (gen * 2 + across) * width
    for n, bit in enumerate(bits):
        first = first + ((learn // bit) % 2) * (width >> (n + 1))
    w_part = lax.dynamic_slice(w_key, (first, core * half), (tall, half)).astype(F32)
    gains = jnp.sum(w_part * total, 1) / lax.dynamic_slice_in_dim(in_gain, first, tall)

    parts, y_parts, offsets = [total.astype(BF16)], [], [0]
    order = list(held.values()) + list(passed.values())
    used = sum(part.shape[0] for part in order)
    place = -(-used // 128) * 128
    for n, bit in enumerate(reversed(bits)):
        block = parts[0] if n == 0 else jnp.concatenate(parts, 0)
        received = across_learn(block, bit)
        y_parts.append(across_learn(parts[-1], 2))
        if n == 0:
            all_rows = pl.pallas_call(
                stack_kernel,
                out_shape=jax.ShapeDtypeStruct((place, packed_width), BF16),
                in_specs=[VMEM] * len(order),
                out_specs=VMEM,
                compiler_params=limit(STACK_MIB),
            )(*order)
            other_rows = across_learn(all_rows, 1)
            gains = gains + across_learn(gains, 1)
            gains = gains[None]
            step = 1
            while step < gens:
                gains = join(gains, swap(gains, "gen", gens, step), (gen // step) % 2)
                step *= 2
            for other_bit in bits[1:]:
                sums = sums + across_learn(sums, other_bit)
            received, y_parts, all_rows, other_rows, gains, sums = barrier(
                (received, y_parts, all_rows, other_rows, gains, sums)
            )
        parts = parts + [received]
        weight = planes >> (bits.index(bit) + 1)
        offsets = offsets + [o ^ weight for o in offsets]
        if n:
            wide = bits[-n]
            gains = join_at(gains, across_learn(gains, wide), (learn // wide) % 2, 1)
    rows_placed, keys_placed = pl.pallas_call(
        place_kernel,
        out_shape=[
            jax.ShapeDtypeStruct((SLOTS * TILE, features), BF16),
            jax.ShapeDtypeStruct((SLOTS * TILE, key_count), BF16),
        ],
        in_specs=[SMEM, VMEM, VMEM],
        out_specs=[VMEM] * 2,
        scratch_shapes=[pltpu.VMEM((SLOTS * TILE, 2 * place), BF16)],
        compiler_params=limit(PLACE_MIB),
    )(learn[None], all_rows, other_rows)
    parts, y_parts, gains, sums, rows_placed, keys_placed = barrier(
        (parts, y_parts, gains, sums, rows_placed, keys_placed)
    )

    y_parts.append(across_learn(parts[-1], 2))
    _, rows_placed = lax.while_loop(
        lambda state: state[0] > 0.5,
        lambda state: (
            jnp.zeros((), F32),
            swap_dense(hidden, grad_keys, w_key, in_gain, destination[:, 0], learners),
        ),
        (sums[0, -1], rows_placed),
    )
    grad_slots = pl.pallas_call(
        slots_kernel,
        out_shape=jax.ShapeDtypeStruct((SLOTS * TILE, features), BF16),
        in_specs=[SMEM, VMEM, VMEM, ANY, VMEM],
        out_specs=VMEM,
        scratch_shapes=[
            pltpu.VMEM((features, key_count), BF16),
            pltpu.VMEM((SLOTS * TILE, features), F32),
            pltpu.SemaphoreType.DMA((strips,)),
        ],
        compiler_params=limit(SLOTS_MIB),
    )(sums[0, -1:], rows_placed, keys_placed, w_key, in_gain_row)
    core_parts = [across_learn(part, 1) for part in parts]
    core_y = [across_learn(part, 1) for part in y_parts[:-1]]
    first = sum(((learn // bit) % 2) * (planes >> (n + 1)) for n, bit in enumerate(bits))
    first = first ^ jnp.asarray(offsets, jnp.int32)
    w_rows = 2 * width
    w_grad = lay_out(
        jnp.concatenate([across * planes + first, core[None]]), parts, core_parts, tall, w_rows
    )
    near = [across_learn(gains, bit) for bit in (bits[0], 2, bits[0] + 2)]
    upper = (learn // bits[0]) % 2
    gains = join_at(
        join_at(gains, near[0], upper, 1), join_at(near[1], near[2], upper, 1), across, 1
    )
    w_grad, y_parts, core_y, gains, sums, grad_slots = barrier(
        (w_grad, y_parts, core_y, gains, sums, grad_slots)
    )
    core_y.append(across_learn(y_parts[-1], 1))
    w_grad = lay_out(
        jnp.concatenate([(1 - across) * planes + first, core[None]]),
        y_parts,
        core_y,
        tall,
        w_rows,
        w_grad,
    )
    return (grad_slots, w_grad, gains.reshape(-1), sums[0, :head])


def solution(mesh):
    return jax.shard_map(
        body,
        mesh=mesh,
        in_specs=(
            P(("gen", "learn"), None),
            P(("gen", "learn"), None),
            P(("gen", "learn")),
            P(("gen", "learn")),
            P(("gen", "learn")),
            P(("gen", "learn"), None),
            P(),
            P(),
            P(),
        ),
        out_specs=(P(("gen", "learn"), None), P("gen", None), P(), P()),
        check_vma=False,
    )
```

```python
import functools

import jax
import jax.numpy as jnp
from jax import lax
from jax.experimental import pallas as pl
from jax.experimental.pallas import tpu as pltpu
from jax.sharding import PartitionSpec as P

TILE = 8
VERSIONS = 4
SLOTS = 64
PACKET = 72
PASSED_ON = 48
TAGS = 128
STRIP = 512
UNROLL = 5
KEYS_MIB, STACK_MIB, PLACE_MIB, SLOTS_MIB = 56, 20, 36, 44


epsilon = 1e-06
clip_ratio = 2.0
staleness = 0.5
BOTH = ("gen", "learn")
F32 = jnp.float32
BF16 = jnp.bfloat16


def to_column(row, size):
    same = lax.broadcasted_iota(jnp.int32, (size, size), 0) == lax.broadcasted_iota(
        jnp.int32, (size, size), 1
    )
    return jnp.sum(jnp.where(same, row, jnp.zeros_like(row)), 1, keepdims=True)


def row_values(per_block, rows):
    shape = (rows, per_block.shape[1])
    own = lax.broadcasted_iota(jnp.int32, shape, 0) // TILE == lax.broadcasted_iota(
        jnp.int32, shape, 1
    )
    return jnp.sum(jnp.where(own, per_block, jnp.zeros_like(per_block)), 1, keepdims=True)


def token_weights(importance_row, len_row, version_row):
    rows = importance_row.shape[1]
    stale_age = VERSIONS - 1 - version_row
    decay_row = jnp.zeros(stale_age.shape, F32)
    for age in range(VERSIONS):
        decay_row = jnp.where(stale_age == age, staleness**age, decay_row)
    inside = lax.broadcasted_iota(jnp.int32, (rows, 1), 0) % TILE < row_values(len_row, rows)
    importance = jnp.minimum(to_column(importance_row, rows), clip_ratio)
    return importance * (row_values(decay_row, rows) * jnp.where(inside, 1.0, 0.0))


def swap(x, axis, size, bit):
    return lax.ppermute(x, axis, [(i, i ^ bit) for i in range(size)])


def butterfly_sum(x, axes, learners=None):
    for axis, size in axes:
        bit = 1
        while bit < size:
            x = x + swap(x, axis, learners or size, bit)
            bit *= 2
    return x


def join_at(mine, other, upper, axis):
    place = lax.broadcasted_iota(jnp.int32, (2,) + (1,) * (mine.ndim - axis), 0)
    return jnp.where(
        place == upper, jnp.expand_dims(mine, axis), jnp.expand_dims(other, axis)
    )


def join(mine, other, upper):
    return join_at(mine, other, upper, 0).reshape((2 * mine.shape[0],) + mine.shape[1:])


def dot_rows(a, b):
    return lax.dot_general(a, b, (((0,), (0,)), ((), ())), preferred_element_type=F32)


VMEM = pl.BlockSpec(memory_space=pltpu.VMEM)
SMEM = pl.BlockSpec(memory_space=pltpu.SMEM)
ANY = pl.BlockSpec(memory_space=pl.ANY)


def keys_kernel(blocks, plan, pieces, index_ref, *refs):
    sources, outs, rests = refs[:9], refs[9 : 9 + blocks], refs[9 + blocks : 9 + 2 * blocks]
    refs = refs[9 + 2 * blocks :]
    main = outs[0].shape[0]
    planes, packet = plan[:2]
    packs, refs = refs[: len(pieces)], refs[len(pieces) :]
    (keys_out, sums_out), held, (w_all, h_all, keys, sems) = refs[:2], refs[2:10], refs[10:]

    def spread(packed, first):
        for pack, (low, high) in zip(packs, pieces):
            pack[:, first] = packed[low:high]

    w_ref = sources[8]
    copies = [
        pltpu.make_async_copy(source, place, sems.at[i])
        for i, (source, place) in enumerate(zip(sources[:8], held))
    ]
    for copy in copies:
        copy.start()
    hidden_ref, len_ref, dest_ref, importance_ref, version_ref, gain_ref, key_gain_ref = held[:7]
    cotangent_ref = held[7]
    rows, features = hidden_ref.shape
    strips = features // STRIP

    def strip(i):
        return pl.ds(pl.multiple_of(i * STRIP, STRIP), STRIP)

    def fetch(i):
        return pltpu.make_async_copy(w_ref.at[strip(i)], w_all.at[strip(i)], sems.at[8 + i])

    for i in range(strips):
        fetch(i).start()
    for copy in copies[1:3]:
        copy.wait()
    place, tags, over, order, many = packet_plan(
        index_ref[blocks], len_ref[...], dest_ref[...], rows, main, *plan
    )
    places = lax.broadcasted_iota(jnp.int32, (planes * packet, rows), 0)
    onehot = (places == place).astype(F32).astype(BF16)
    places = lax.broadcasted_iota(jnp.int32, (rows, rows), 0)
    squeeze = (places == order).astype(F32).astype(BF16)
    for copy in copies[3:]:
        copy.wait()
    weight = token_weights(importance_ref[...], len_ref[...], version_ref[...])
    copies[0].wait()

    def squares(i, total):
        part = hidden_ref[:, strip(i)]
        packed = jnp.dot(onehot, part, preferred_element_type=F32).astype(BF16)
        spread(packed, strip(i))
        x = part.astype(F32)
        return total + jnp.sum(x * x, 1, keepdims=True)

    square_sum = lax.fori_loop(
        0, strips, squares, jnp.zeros((rows, 1), F32), unroll=UNROLL
    )
    packed = jnp.dot(onehot, tags, preferred_element_type=F32).astype(BF16)
    spread(packed, slice(features, features + TAGS))
    inv = lax.rsqrt(square_sum / features + epsilon)
    keys[...] = jnp.zeros_like(keys)

    def project(i, carry):
        h = (hidden_ref[:, strip(i)].astype(F32) * inv * gain_ref[:, strip(i)]).astype(BF16)
        h_all[:, strip(i)] = jnp.dot(squeeze, h, preferred_element_type=F32).astype(BF16)
        fetch(i).wait()
        keys[...] += jnp.dot(h, w_all[strip(i), :], preferred_element_type=F32)
        return carry

    lax.fori_loop(0, strips, project, 0, unroll=UNROLL)
    width = outs[0].shape[1] - keys.shape[1]
    for k in range(blocks):
        columns = pl.ds(pl.multiple_of(index_ref[k] * width, width), width)
        outs[k][:, :width] = h_all[:main, columns]
        rests[k][:, :width] = h_all[main:, columns]
    head = key_gain_ref.shape[1]
    kgain = jnp.zeros((1, head), F32)
    for a in range(keys.shape[1] // head):
        span = slice(a * head, (a + 1) * head)
        key = keys[:, span]
        scale = lax.rsqrt(jnp.mean(key * key, 1, keepdims=True) + epsilon)
        upstream = (cotangent_ref[:, span].astype(F32) * weight).astype(BF16).astype(F32)
        kgain = kgain + jnp.sum(upstream * key * scale, 0, keepdims=True)
        scaled = upstream * key_gain_ref[...]
        grad = scale * scaled - key * (scale * scale * scale) * jnp.mean(
            scaled * key, 1, keepdims=True
        )
        keys_out[:, span] = grad.astype(BF16)
    sums_out[:, :head] = kgain
    sums_out[:, head : 2 * head] = jnp.broadcast_to(over, (1, head))
    sums_out[:, 2 * head :] = jnp.broadcast_to(many, (1, head))
    packed = jnp.dot(squeeze, keys_out[...], preferred_element_type=F32).astype(BF16)
    for k in range(blocks):
        outs[k][:, width:] = packed[:main]
        rests[k][:, width:] = packed[main:]
    packed = jnp.dot(onehot, keys_out[...], preferred_element_type=F32).astype(BF16)
    spread(packed, slice(features + TAGS, features + TAGS + keys.shape[1]))


def packet_plan(learn, len_row, dest_row, rows, main, planes, packet, passed_on, capacity):
    tiles = dest_row.shape[1]
    dest_column = to_column(dest_row, tiles)
    shape = (tiles, tiles)
    earlier = lax.broadcasted_iota(jnp.int32, shape, 0) < lax.broadcasted_iota(jnp.int32, shape, 1)
    alike = earlier & (dest_column == dest_row)
    rank_row = jnp.sum(jnp.where(alike, 1, 0), 0, keepdims=True)
    shape = (tiles, rows)
    token = lax.broadcasted_iota(jnp.int32, shape, 1)
    own = token // TILE == lax.broadcasted_iota(jnp.int32, shape, 0)
    dest = jnp.sum(jnp.where(own, dest_column, 0), 0, keepdims=True)
    length = jnp.sum(jnp.where(own, to_column(len_row, tiles), 0), 0, keepdims=True)
    valid = token[:1] % TILE < length
    apart = dest ^ learn
    kind = jnp.where(valid, (apart // 4) * 2 + (apart // 2) % 2, 2 * planes)
    kinds = lax.broadcasted_iota(jnp.int32, (2 * planes, 1), 0)
    member = kind == kinds
    shape = (rows, rows)
    before = lax.broadcasted_iota(jnp.int32, shape, 0) < lax.broadcasted_iota(jnp.int32, shape, 1)
    counted = jnp.where(member, 1.0, 0.0)
    ahead = jnp.dot(
        counted.astype(BF16),
        jnp.where(before, 1.0, 0.0).astype(BF16),
        preferred_element_type=F32,
    ).astype(jnp.int32)
    count = jnp.sum(counted, 1, keepdims=True).astype(jnp.int32)
    start = (kinds // 2) * packet + jnp.where(kinds % 2 == 1, packet - count, 0)
    position = jnp.sum(jnp.where(member, ahead + start, 0), 0, keepdims=True)
    position = jnp.where(valid, position, -1)
    order = jnp.where(valid, jnp.sum(ahead, 0, keepdims=True), -1)
    many = jnp.where(jnp.sum(count, 0, keepdims=True) > main, 1.0, 0.0)
    plane_of = lax.broadcasted_iota(jnp.int32, (2 * planes, planes), 0) // 2
    same_plane = plane_of == lax.broadcasted_iota(jnp.int32, (2 * planes, planes), 1)
    together = jnp.sum(jnp.where(same_plane, count, 0), 0, keepdims=True)
    too_many = jnp.where((kinds % 2 == 1) & (count > passed_on), 1.0, 0.0)
    over = jnp.max(jnp.where(together > packet, 1.0, 0.0), 1, keepdims=True) + jnp.max(
        too_many, 0, keepdims=True
    )
    lane = lax.broadcasted_iota(jnp.int32, (rows, TAGS), 1)
    line = lax.broadcasted_iota(jnp.int32, (rows, TAGS), 0) % TILE
    slot = learn * capacity + row_values(rank_row, rows)
    tags = jnp.where(lane == 0, row_values(dest_row, rows) + 1, jnp.where(lane == 1, slot, line))
    tags = jnp.where(lane < 3, tags, 0)
    return position, tags.astype(F32).astype(BF16), over, order, many


def stack_kernel(*refs):
    out, used = refs[-1], 0
    for part in refs[:-1]:
        out[used : used + part.shape[0], :] = part[...]
        used += part.shape[0]


def place_kernel(me_ref, *refs):
    sources, (rows_out, keys_out, held, chosen, sems) = refs[:4], refs[4:]
    slots, features = rows_out.shape
    copies, used = [], 0
    for i, source in enumerate(sources):
        place = held.at[pl.ds(used, source.shape[0])]
        copies.append(pltpu.make_async_copy(source, place, sems.at[i]))
        copies[-1].start()
        used += source.shape[0]
    if used < held.shape[0]:
        held[used:, :] = jnp.zeros((held.shape[0] - used, held.shape[1]), BF16)
    for copy in copies:
        copy.wait()
    tags = held[:, features : features + TAGS].astype(F32).T.astype(jnp.int32)
    target = jnp.where(tags[0:1] == me_ref[0] + 1, tags[1:2] * TILE + tags[2:3], -1)
    places = lax.broadcasted_iota(jnp.int32, (slots, held.shape[0]), 0)
    chosen[...] = (places == target).astype(F32).astype(BF16)

    def pick(columns):
        return jnp.dot(
            chosen[...], held[:, columns], preferred_element_type=F32
        ).astype(BF16)

    def put(i, carry):
        strip = pl.ds(pl.multiple_of(i * STRIP, STRIP), STRIP)
        rows_out[:, strip] = pick(strip)
        return carry

    lax.fori_loop(0, features // STRIP, put, 0, unroll=UNROLL)
    keys_out[...] = pick(slice(features + TAGS, features + TAGS + keys_out.shape[1]))


def slots_kernel(over_ref, rows_ref, keys_ref, w_ref, gain_ref, out_ref, w_all, grad, sems):
    slots, features = out_ref.shape
    strips = features // STRIP

    def strip(i):
        return pl.ds(pl.multiple_of(i * STRIP, STRIP), STRIP)

    def fetch(i):
        return pltpu.make_async_copy(w_ref.at[strip(i)], w_all.at[strip(i)], sems.at[i])

    for i in range(strips):
        fetch(i).start()

    def back(i, total):
        rows = rows_ref[:, strip(i)].astype(F32)
        fetch(i).wait()
        g = gain_ref[:, strip(i)] * lax.dot_general(
            keys_ref[...], w_all[strip(i), :], (((1,), (1,)), ((), ())), preferred_element_type=F32
        )
        grad[:, strip(i)] = g
        squares, products = total
        return (
            squares + jnp.sum(rows * rows, 1, keepdims=True),
            products + jnp.sum(g * rows, 1, keepdims=True),
        )

    zero = jnp.zeros((slots, 1), F32)
    squares, products = lax.fori_loop(0, strips, back, (zero, zero), unroll=UNROLL)
    inv = lax.rsqrt(squares / features + epsilon)
    mean = products * inv / features

    def finish(i, carry):
        normed = rows_ref[:, strip(i)].astype(F32) * inv
        out_ref[:, strip(i)] = (inv * (grad[:, strip(i)] - normed * mean)).astype(BF16)
        return carry

    lax.fori_loop(0, strips, finish, 0, unroll=UNROLL)

    @pl.when(over_ref[0] > 0.5)
    def _():
        out_ref[...] = rows_ref[...]


def output_kernel(sizes, index_ref, *refs):
    count = len(sizes)
    mine, others, out_ref = refs[:count], refs[count : 2 * count], refs[-1]
    half = mine[0].shape[1]
    step = pl.program_id(0)
    core = index_ref[sum(sizes)]
    columns = pl.ds(pl.multiple_of(core * half, half), half)
    other_columns = pl.ds(pl.multiple_of((1 - core) * half, half), half)
    first = 0
    for k, size in enumerate(sizes):

        @pl.when((step >= first) & (step < first + size))
        def _():
            out_ref[:, columns] = mine[k][...].astype(F32)
            out_ref[:, other_columns] = others[k][...].astype(F32)

        first += size


def lay_out(index, mine, others, tall, rows, filled=None):
    half = mine[0].shape[1]
    sizes = [part.shape[0] // tall for part in mine]

    def spec(k):
        first, size = sum(sizes[:k]), sizes[k]
        return pl.BlockSpec((tall, half), lambda i, ids: (jnp.clip(i - first, 0, size - 1), 0))

    specs = [spec(k) for k in range(len(sizes))]
    more = [] if filled is None else [filled]
    return pl.pallas_call(
        functools.partial(output_kernel, sizes),
        out_shape=jax.ShapeDtypeStruct((rows, 2 * half), F32),
        grid_spec=pltpu.PrefetchScalarGridSpec(
            num_scalar_prefetch=1,
            grid=(sum(sizes),),
            in_specs=specs + specs + [ANY] * len(more),
            out_specs=pl.BlockSpec((tall, 2 * half), lambda i, ids: (ids[i], 0)),
        ),
        input_output_aliases={1 + 2 * len(sizes): 0} if more else {},
        compiler_params=pltpu.CompilerParams(vmem_limit_bytes=24 << 20),
    )(index, *mine, *others, *more)


def swap_dense(hidden, grad_keys, w_key, in_gain, dest_column, learners):
    x_float = hidden.astype(F32)
    inv_rms = lax.rsqrt(jnp.mean(x_float * x_float, -1, keepdims=True) + epsilon)
    normed = x_float * inv_rms
    grad_normed = in_gain * lax.dot_general(
        grad_keys, w_key, (((1,), (1,)), ((), ())), preferred_element_type=F32
    )
    grad_input = inv_rms * (
        grad_normed - normed * jnp.mean(grad_normed * normed, -1, keepdims=True)
    )
    onehot = (dest_column[:, None] == jnp.arange(learners, dtype=jnp.int32)[None, :]).astype(
        jnp.int32
    )
    slot_rank = jnp.sum((jnp.cumsum(onehot, 0) - onehot) * onehot, 1)
    target = dest_column * (SLOTS // learners) + slot_rank
    rows_to = (target[:, None] * TILE + jnp.arange(TILE, dtype=jnp.int32)[None, :]).reshape(-1)
    place = jnp.arange(SLOTS * TILE, dtype=jnp.int32)[:, None]
    spread = jnp.dot(
        (rows_to[None, :] == place).astype(BF16),
        grad_input.astype(BF16),
        preferred_element_type=F32,
    )
    return lax.all_to_all(spread.astype(BF16), "learn", split_axis=0, concat_axis=0, tiled=True)


def body(hidden, cotangent, importance, block_len, version, destination, w_key, in_gain, key_gain):
    learners, gens = lax.axis_size("learn"), lax.axis_size("gen")
    gen, learn = lax.axis_index("gen"), lax.axis_index("learn")
    core, across = learn % 2, (learn // 2) % 2
    capacity = SLOTS // learners
    planes = learners // 4
    packet = min(PACKET, 4 * capacity * TILE)
    passed_on = min(PASSED_ON, 2 * capacity * TILE)
    rows, features = hidden.shape
    main = rows * 3 // 4
    key_count = cotangent.shape[1]
    head = key_gain.shape[0]
    strips = features // STRIP
    blocks = 2 * gens
    width = features // blocks
    half = key_count // 2

    def limit(mebibytes):
        return pltpu.CompilerParams(vmem_limit_bytes=mebibytes << 20)


    front = packet - passed_on
    pieces = []
    for k in range(planes):
        cuts = (0, front, packet) if k in (0, planes - 1) else (0, packet)
        pieces += [(k * packet + low, k * packet + high) for low, high in zip(cuts, cuts[1:])]
    packed_width = features + TAGS + key_count
    steps = [(step, dy) for step in range(gens) for dy in range(2)]
    wanted = [((gen + step) % gens) * 2 + (across ^ dy) for step, dy in steps]
    in_gain_row = in_gain[None, :]
    tiles = block_len.shape[0]
    made = pl.pallas_call(
        functools.partial(
            keys_kernel, blocks, (planes, packet, passed_on, capacity), pieces
        ),
        out_shape=[jax.ShapeDtypeStruct((main, width + key_count), BF16)] * blocks
        + [jax.ShapeDtypeStruct((rows - main, width + key_count), BF16)] * blocks
        + [jax.ShapeDtypeStruct((high - low, packed_width), BF16) for low, high in pieces]
        + [
            jax.ShapeDtypeStruct((rows, key_count), BF16),
            jax.ShapeDtypeStruct((1, 3 * head), F32),
        ],
        in_specs=[SMEM] + [ANY] * 9,
        out_specs=[VMEM] * (2 * blocks + len(pieces) + 2),
        scratch_shapes=[
            pltpu.VMEM((rows, features), BF16),
            pltpu.VMEM((1, tiles), jnp.int32),
            pltpu.VMEM((1, tiles), jnp.int32),
            pltpu.VMEM((1, rows), F32),
            pltpu.VMEM((1, tiles), jnp.int32),
            pltpu.VMEM((1, features), F32),
            pltpu.VMEM((1, head), F32),
            pltpu.VMEM((rows, key_count), BF16),
            pltpu.VMEM((features, key_count), BF16),
            pltpu.VMEM((rows, features), BF16),
            pltpu.VMEM((rows, key_count), F32),
            pltpu.SemaphoreType.DMA((8 + strips,)),
        ],
        compiler_params=limit(KEYS_MIB),
        cost_estimate=pl.CostEstimate(
            flops=2 * rows * features * key_count, bytes_accessed=16 << 20, transcendentals=0
        ),
    )(
        jnp.stack(wanted + [learn]),
        hidden,
        block_len[None, :],
        destination[:, 0][None, :],
        importance[None, :],
        version[None, :],
        in_gain_row,
        key_gain[None, :],
        cotangent,
        w_key,
    )
    operands, rests, made = made[:blocks], made[blocks : 2 * blocks], made[2 * blocks :]
    packs, (grad_keys, sums) = made[: len(pieces)], made[len(pieces) :]

    def gather(k, operands):
        step, dy = steps[k]
        pairs = [
            (p * learners + j, ((p + step) % gens) * learners + (j ^ (2 * dy)))
            for p in range(gens)
            for j in range(learners)
        ]
        return lax.ppermute(operands[k], BOTH, pairs)

    def across_learn(part, bit):
        return swap(part, "learn", learners, bit)

    def over_y(part):
        return across_learn(part[part.shape[0] - passed_on :], 2)

    def products(part):
        keys = lax.dynamic_slice_in_dim(part, width + core * half, half, 1)
        return dot_rows(part[:, :width], keys)

    barrier = lax.optimization_barrier
    direct = [k for k, (step, dy) in enumerate(steps) if (step > 0) + dy == 1]
    diagonal = [k for k, (step, dy) in enumerate(steps) if (step > 0) + dy == 2]
    last = planes - 1
    held, passed = {0: packs[1], planes: packs[0]}, {}

    def add_products(total, parts):
        for part in parts:
            total = total + products(part) + products(across_learn(part, 1))
        return total

    bits = [4 << b for b in range(planes.bit_length() - 1)]

    def halve(total, bit):
        upper = (learn // bit) % 2
        tall = total.shape[0] // 2
        sent = lax.dynamic_slice_in_dim(total, (1 - upper) * tall, tall, 0).astype(BF16)
        kept = lax.dynamic_slice_in_dim(total, upper * tall, tall, 0)
        return kept + across_learn(sent, bit).astype(F32)

    def stack(parts):
        return pl.pallas_call(
            stack_kernel,
            out_shape=jax.ShapeDtypeStruct(
                (sum(part.shape[0] for part in parts), packed_width), BF16
            ),
            in_specs=[VMEM] * len(parts),
            out_specs=VMEM,
            compiler_params=limit(STACK_MIB),
        )(*parts)

    gathered = [gather(k, operands) for k in direct + diagonal]
    for k in range(1, last):
        held[k] = across_learn(packs[1 + k], 4 * k)
    gathered, held, packs = barrier((gathered, held, packs))

    total = add_products(0.0, [operands[0], *gathered])
    held[last] = across_learn(packs[-1], 4 * last)
    passed[0] = over_y(held[0])
    passed[1] = over_y(held[1])
    total, held, passed, packs = barrier((total, held, passed, packs))

    for n, bit in enumerate(bits):
        total = halve(total, bit)
        if n == 0:
            held[planes + 1] = across_learn(packs[-2], 4 * last)
            for k in range(2, last):
                passed[k] = over_y(held[k])
            sums = butterfly_sum(sums, (("gen", gens),))
            sums = butterfly_sum(sums, (("learn", 4),), learners)
        if n == 1:
            stacked = stack(list(held.values()) + list(passed.values()))
            passed[last] = over_y(held[last])
            for other_bit in bits:
                sums = sums + across_learn(sums, other_bit)
            total, passed, stacked, sums = barrier((total, passed, stacked, sums))
        else:
            total, passed, held, sums = barrier((total, passed, held, sums))

    def add_rests(state):
        total = add_products(0.0, [rests[0]] + [gather(k, rests) for k in range(1, blocks)])
        for bit in bits:
            total = halve(total, bit)
        return jnp.zeros((), F32), state[1] + total

    _, total = lax.while_loop(lambda state: state[0] > 0.5, add_rests, (sums[0, -1], total))

    tall = total.shape[0]
    first = (gen * 2 + across) * width
    for n, bit in enumerate(bits):
        first = first + ((learn // bit) % 2) * (width >> (n + 1))
    w_part = lax.dynamic_slice(w_key, (first, core * half), (tall, half)).astype(F32)
    gains = jnp.sum(w_part * total, 1) / lax.dynamic_slice_in_dim(in_gain, first, tall)

    parts, y_parts, offsets = [total.astype(BF16)], [], [0]
    for n, bit in enumerate(reversed(bits)):
        block = parts[0] if n == 0 else jnp.concatenate(parts, 0)
        received = across_learn(block, bit)
        y_parts.append(across_learn(parts[-1], 2))
        if n == 0:
            other_stacked = across_learn(stacked, 1)
            other_passed = across_learn(passed[last], 1)
            gains = gains + across_learn(gains, 1)
            gains = gains[None]
            step = 1
            while step < gens:
                gains = join(gains, swap(gains, "gen", gens, step), (gen // step) % 2)
                step *= 2
            received, y_parts, other_stacked, other_passed, gains = barrier(
                (received, y_parts, other_stacked, other_passed, gains)
            )
        parts = parts + [received]
        weight = planes >> (bits.index(bit) + 1)
        offsets = offsets + [o ^ weight for o in offsets]
        if n:
            wide = bits[-n]
            gains = join_at(gains, across_learn(gains, wide), (learn // wide) % 2, 1)
    place = -(-2 * (stacked.shape[0] + passed_on) // 128) * 128
    rows_placed, keys_placed = pl.pallas_call(
        place_kernel,
        out_shape=[
            jax.ShapeDtypeStruct((SLOTS * TILE, features), BF16),
            jax.ShapeDtypeStruct((SLOTS * TILE, key_count), BF16),
        ],
        in_specs=[SMEM] + [ANY] * 4,
        out_specs=[VMEM] * 2,
        scratch_shapes=[
            pltpu.VMEM((place, packed_width), BF16),
            pltpu.VMEM((SLOTS * TILE, place), BF16),
            pltpu.SemaphoreType.DMA((4,)),
        ],
        compiler_params=limit(PLACE_MIB),
    )(learn[None], stacked, passed[last], other_stacked, other_passed)
    parts, y_parts, gains, sums, rows_placed, keys_placed = barrier(
        (parts, y_parts, gains, sums, rows_placed, keys_placed)
    )

    y_parts.append(across_learn(parts[-1], 2))
    _, rows_placed = lax.while_loop(
        lambda state: state[0] > 0.5,
        lambda state: (
            jnp.zeros((), F32),
            swap_dense(hidden, grad_keys, w_key, in_gain, destination[:, 0], learners),
        ),
        (sums[0, head], rows_placed),
    )
    grad_slots = pl.pallas_call(
        slots_kernel,
        out_shape=jax.ShapeDtypeStruct((SLOTS * TILE, features), BF16),
        in_specs=[SMEM, VMEM, VMEM, ANY, VMEM],
        out_specs=VMEM,
        scratch_shapes=[
            pltpu.VMEM((features, key_count), BF16),
            pltpu.VMEM((SLOTS * TILE, features), F32),
            pltpu.SemaphoreType.DMA((strips,)),
        ],
        compiler_params=limit(SLOTS_MIB),
    )(sums[0, head : head + 1], rows_placed, keys_placed, w_key, in_gain_row)
    core_parts = [across_learn(part, 1) for part in parts]
    core_y = [across_learn(part, 1) for part in y_parts[:-1]]
    first = sum(((learn // bit) % 2) * (planes >> (n + 1)) for n, bit in enumerate(bits))
    first = first ^ jnp.asarray(offsets, jnp.int32)
    w_rows = 2 * width
    w_grad = lay_out(
        jnp.concatenate([across * planes + first, core[None]]), parts, core_parts, tall, w_rows
    )
    near = [across_learn(gains, bit) for bit in (bits[0], 2, bits[0] + 2)]
    upper = (learn // bits[0]) % 2
    gains = join_at(
        join_at(gains, near[0], upper, 1), join_at(near[1], near[2], upper, 1), across, 1
    )
    w_grad, y_parts, core_y, gains, sums, grad_slots = barrier(
        (w_grad, y_parts, core_y, gains, sums, grad_slots)
    )
    core_y.append(across_learn(y_parts[-1], 1))
    w_grad = lay_out(
        jnp.concatenate([(1 - across) * planes + first, core[None]]),
        y_parts,
        core_y,
        tall,
        w_rows,
        w_grad,
    )
    return (grad_slots, w_grad, gains.reshape(-1), sums[0, :head])


def solution(mesh):
    return jax.shard_map(
        body,
        mesh=mesh,
        in_specs=(
            P(("gen", "learn"), None),
            P(("gen", "learn"), None),
            P(("gen", "learn")),
            P(("gen", "learn")),
            P(("gen", "learn")),
            P(("gen", "learn"), None),
            P(),
            P(),
            P(),
        ),
        out_specs=(P(("gen", "learn"), None), P("gen", None), P(), P()),
        check_vma=False,
    )
```

```python
import functools

import jax
import jax.numpy as jnp
from jax import lax
from jax.experimental import pallas as pl
from jax.experimental.pallas import tpu as pltpu
from jax.sharding import PartitionSpec as P

TILE = 8
VERSIONS = 4
SLOTS = 64
PACKET = 72
PASSED_ON = 48
TAGS = 128
STRIP = 512
UNROLL = 5
EXTRA = 16
CHUNK = 64
KEYS_MIB, PRODUCTS_MIB, FINISH_MIB, STACK_MIB, PLACE_MIB, SLOTS_MIB = 56, 20, 8, 20, 36, 44


epsilon = 1e-06
clip_ratio = 2.0
staleness = 0.5
BOTH = ("gen", "learn")
F32 = jnp.float32
BF16 = jnp.bfloat16


def to_column(row, size):
    same = lax.broadcasted_iota(jnp.int32, (size, size), 0) == lax.broadcasted_iota(
        jnp.int32, (size, size), 1
    )
    return jnp.sum(jnp.where(same, row, jnp.zeros_like(row)), 1, keepdims=True)


def row_values(per_block, rows):
    shape = (rows, per_block.shape[1])
    own = lax.broadcasted_iota(jnp.int32, shape, 0) // TILE == lax.broadcasted_iota(
        jnp.int32, shape, 1
    )
    return jnp.sum(jnp.where(own, per_block, jnp.zeros_like(per_block)), 1, keepdims=True)


def token_weights(importance_row, len_row, version_row):
    rows = importance_row.shape[1]
    stale_age = VERSIONS - 1 - version_row
    decay_row = jnp.zeros(stale_age.shape, F32)
    for age in range(VERSIONS):
        decay_row = jnp.where(stale_age == age, staleness**age, decay_row)
    inside = lax.broadcasted_iota(jnp.int32, (rows, 1), 0) % TILE < row_values(len_row, rows)
    importance = jnp.minimum(to_column(importance_row, rows), clip_ratio)
    return importance * (row_values(decay_row, rows) * jnp.where(inside, 1.0, 0.0))


def swap(x, axis, size, bit):
    return lax.ppermute(x, axis, [(i, i ^ bit) for i in range(size)])


def butterfly_sum(x, axes, learners=None):
    for axis, size in axes:
        bit = 1
        while bit < size:
            x = x + swap(x, axis, learners or size, bit)
            bit *= 2
    return x


def join_at(mine, other, upper, axis):
    place = lax.broadcasted_iota(jnp.int32, (2,) + (1,) * (mine.ndim - axis), 0)
    return jnp.where(
        place == upper, jnp.expand_dims(mine, axis), jnp.expand_dims(other, axis)
    )


def join(mine, other, upper):
    return join_at(mine, other, upper, 0).reshape((2 * mine.shape[0],) + mine.shape[1:])


def dot_rows(a, b):
    return lax.dot_general(a, b, (((0,), (0,)), ((), ())), preferred_element_type=F32)


VMEM = pl.BlockSpec(memory_space=pltpu.VMEM)
SMEM = pl.BlockSpec(memory_space=pltpu.SMEM)
ANY = pl.BlockSpec(memory_space=pl.ANY)


def keys_kernel(blocks, plan, pieces, index_ref, *refs):
    sources, outs, rests = refs[:9], refs[9 : 9 + blocks], refs[9 + blocks : 9 + 2 * blocks]
    refs = refs[9 + 2 * blocks :]
    main = outs[0].shape[0]
    planes, packet = plan[:2]
    packs, refs = refs[: len(pieces)], refs[len(pieces) :]
    (keys_out, sums_out), held, (w_all, h_all, keys, sums, sems) = refs[:2], refs[2:10], refs[10:]

    def spread(packed, first):
        for pack, (low, high) in zip(packs, pieces):
            pack[: high - low, first] = packed[low:high]

    w_ref = sources[8]
    copies = [
        pltpu.make_async_copy(source, place, sems.at[i])
        for i, (source, place) in enumerate(zip(sources[:8], held))
    ]
    for copy in copies:
        copy.start()
    hidden_ref, len_ref, dest_ref, importance_ref, version_ref, gain_ref, key_gain_ref = held[:7]
    cotangent_ref = held[7]
    rows, features = hidden_ref.shape
    strips = features // STRIP

    def strip(i):
        return pl.ds(pl.multiple_of(i * STRIP, STRIP), STRIP)

    def fetch(i):
        return pltpu.make_async_copy(w_ref.at[strip(i)], w_all.at[strip(i)], sems.at[8 + i])

    for i in range(strips):
        fetch(i).start()
    for copy in copies[1:3]:
        copy.wait()
    place, tags, over, order, many = packet_plan(
        index_ref[blocks], len_ref[...], dest_ref[...], rows, main, *plan
    )
    places = lax.broadcasted_iota(jnp.int32, (planes * packet, rows), 0)
    onehot = (places == place).astype(F32).astype(BF16)
    places = lax.broadcasted_iota(jnp.int32, (rows, rows), 0)
    squeeze = (places == order).astype(F32).astype(BF16)
    for copy in copies[3:]:
        copy.wait()
    weight = token_weights(importance_ref[...], len_ref[...], version_ref[...])
    copies[0].wait()

    sums[...] = jnp.zeros_like(sums)
    spans = [slice(k, k + STRIP) for k in range(0, features, STRIP)]
    for span in spans:
        packed = jnp.dot(onehot, hidden_ref[:, span], preferred_element_type=F32).astype(BF16)
        spread(packed, span)

        def add(at):
            x = hidden_ref[at, span].astype(F32)
            sums[at, :] += lane_sums(x * x)

        over_chunks(rows, add)
    packed = jnp.dot(onehot, tags, preferred_element_type=F32).astype(BF16)
    spread(packed, slice(features, features + TAGS))
    inv = lax.rsqrt(jnp.sum(sums[...], 1, keepdims=True) / features + epsilon)
    sums[...] = jnp.broadcast_to(inv, sums.shape)
    for i, span in enumerate(spans):
        gain = gain_ref[:, span]

        def scale(at):
            by = jnp.concatenate([sums[at, :]] * (STRIP // 128), 1)
            hidden_ref[at, span] = (hidden_ref[at, span].astype(F32) * by * gain).astype(BF16)

        over_chunks(rows, scale)
        h = hidden_ref[:, span]
        h_all[:, span] = jnp.dot(squeeze, h, preferred_element_type=F32).astype(BF16)
        fetch(i).wait()
        product = jnp.dot(h, w_all[span, :], preferred_element_type=F32)
        keys[...] = keys[...] + product if i else product

    width = outs[0].shape[1] - keys.shape[1]
    for k in range(blocks):
        columns = pl.ds(pl.multiple_of(index_ref[k] * width, width), width)
        outs[k][:, :width] = h_all[:main, columns]
        rests[k][:, :width] = h_all[main:, columns]
    head = key_gain_ref.shape[1]
    kgain = jnp.zeros((1, head), F32)
    for a in range(keys.shape[1] // head):
        span = slice(a * head, (a + 1) * head)
        key = keys[:, span]
        scale = lax.rsqrt(jnp.mean(key * key, 1, keepdims=True) + epsilon)
        upstream = (cotangent_ref[:, span].astype(F32) * weight).astype(BF16).astype(F32)
        kgain = kgain + jnp.sum(upstream * key * scale, 0, keepdims=True)
        scaled = upstream * key_gain_ref[...]
        grad = scale * scaled - key * (scale * scale * scale) * jnp.mean(
            scaled * key, 1, keepdims=True
        )
        keys_out[:, span] = grad.astype(BF16)
    sums_out[:, :head] = kgain
    sums_out[:, head : 2 * head] = jnp.broadcast_to(over, (1, head))
    sums_out[:, 2 * head :] = jnp.broadcast_to(many, (1, head))
    packed = jnp.dot(squeeze, keys_out[...], preferred_element_type=F32).astype(BF16)
    for k in range(blocks):
        outs[k][:, width:] = packed[:main]
        rests[k][:, width:] = packed[main:]
    packed = jnp.dot(onehot, keys_out[...], preferred_element_type=F32).astype(BF16)
    spread(packed, slice(features + TAGS, features + TAGS + keys.shape[1]))
    value = kgain
    line = lax.broadcasted_iota(jnp.int32, (EXTRA, head // 2), 0)
    split = jnp.where(line == 6, over, jnp.where(line == 7, many, 0.0))
    for i in range(3):
        term = value.astype(BF16).astype(F32)
        value = value - term
        split = jnp.where(line == 2 * i, term[:, : head // 2], split)
        split = jnp.where(line == 2 * i + 1, term[:, head // 2 :], split)
    split = jnp.concatenate([jnp.zeros((EXTRA, TAGS - head // 2), F32), split], 1)
    for pack in packs[2:]:
        beside = pack[:EXTRA, features : features + TAGS].astype(F32) + split
        pack[:EXTRA, features : features + TAGS] = beside.astype(BF16)


def packet_plan(learn, len_row, dest_row, rows, main, planes, packet, passed_on, capacity):
    tiles = dest_row.shape[1]
    dest_column = to_column(dest_row, tiles)
    shape = (tiles, tiles)
    earlier = lax.broadcasted_iota(jnp.int32, shape, 0) < lax.broadcasted_iota(jnp.int32, shape, 1)
    alike = earlier & (dest_column == dest_row)
    rank_row = jnp.sum(jnp.where(alike, 1, 0), 0, keepdims=True)
    shape = (tiles, rows)
    token = lax.broadcasted_iota(jnp.int32, shape, 1)
    own = token // TILE == lax.broadcasted_iota(jnp.int32, shape, 0)
    dest = jnp.sum(jnp.where(own, dest_column, 0), 0, keepdims=True)
    length = jnp.sum(jnp.where(own, to_column(len_row, tiles), 0), 0, keepdims=True)
    valid = token[:1] % TILE < length
    apart = dest ^ learn
    kind = jnp.where(valid, (apart // 4) * 2 + (apart // 2) % 2, 2 * planes)
    kinds = lax.broadcasted_iota(jnp.int32, (2 * planes, 1), 0)
    member = kind == kinds
    shape = (rows, rows)
    before = lax.broadcasted_iota(jnp.int32, shape, 0) < lax.broadcasted_iota(jnp.int32, shape, 1)
    counted = jnp.where(member, 1.0, 0.0)
    ahead = jnp.dot(
        counted.astype(BF16),
        jnp.where(before, 1.0, 0.0).astype(BF16),
        preferred_element_type=F32,
    ).astype(jnp.int32)
    count = jnp.sum(counted, 1, keepdims=True).astype(jnp.int32)
    start = (kinds // 2) * packet + jnp.where(kinds % 2 == 1, packet - count, 0)
    position = jnp.sum(jnp.where(member, ahead + start, 0), 0, keepdims=True)
    position = jnp.where(valid, position, -1)
    order = jnp.where(valid, jnp.sum(ahead, 0, keepdims=True), -1)
    many = jnp.where(jnp.sum(count, 0, keepdims=True) > main, 1.0, 0.0)
    plane_of = lax.broadcasted_iota(jnp.int32, (2 * planes, planes), 0) // 2
    same_plane = plane_of == lax.broadcasted_iota(jnp.int32, (2 * planes, planes), 1)
    together = jnp.sum(jnp.where(same_plane, count, 0), 0, keepdims=True)
    too_many = jnp.where((kinds % 2 == 1) & (count > passed_on), 1.0, 0.0)
    over = jnp.max(jnp.where(together > packet, 1.0, 0.0), 1, keepdims=True) + jnp.max(
        too_many, 0, keepdims=True
    )
    lane = lax.broadcasted_iota(jnp.int32, (rows, TAGS), 1)
    line = lax.broadcasted_iota(jnp.int32, (rows, TAGS), 0) % TILE
    slot = learn * capacity + row_values(rank_row, rows)
    tags = jnp.where(lane == 0, row_values(dest_row, rows) + 1, jnp.where(lane == 1, slot, line))
    tags = jnp.where(lane < 3, tags, 0)
    return position, tags.astype(F32).astype(BF16), over, order, many


def products_kernel(count, core_ref, *refs):
    sources, (out_ref, parts, sems) = refs[:count], refs[count:]
    width, half = out_ref.shape
    tall = width // 5
    keys = pl.ds(pl.multiple_of(width + core_ref[0] * half, half), half)
    copies = [
        pltpu.make_async_copy(source, parts.at[k], sems.at[k]) for k, source in enumerate(sources)
    ]
    for copy in copies:
        copy.start()
    for k, copy in enumerate(copies):
        copy.wait()

        def block(i, carry):
            rows = pl.ds(pl.multiple_of(i * tall, tall), tall)
            product = lax.dot_general(
                parts[k, :, rows],
                parts[k, :, keys],
                (((0,), (0,)), ((), ())),
                preferred_element_type=F32,
            )
            out_ref[rows, :] = product + out_ref[rows, :] if k else product
            return carry

        lax.fori_loop(0, 5, block, 0, unroll=True)


def finish_kernel(
    index_ref, total_ref, w_ref, gain_ref, block_out, gains_out, w_part, gain, sems
):
    tall, half = total_ref.shape
    rows = pl.ds(pl.multiple_of(index_ref[0] * tall, tall), tall)
    columns = pl.ds(pl.multiple_of(index_ref[1] * half, half), half)
    fetch_w = pltpu.make_async_copy(w_ref.at[rows, columns], w_part, sems.at[0])
    fetch_gain = pltpu.make_async_copy(gain_ref, gain, sems.at[1])
    fetch_w.start()
    fetch_gain.start()
    total = total_ref[...]
    block_out[...] = total.astype(BF16)
    fetch_gain.wait()
    fetch_w.wait()
    sums = jnp.sum(w_part[...].astype(F32) * total, 1, keepdims=True)
    shape = (tall, tall)
    same = lax.broadcasted_iota(jnp.int32, shape, 0) == lax.broadcasted_iota(jnp.int32, shape, 1)
    gains_out[...] = jnp.sum(jnp.where(same, sums, 0.0), 0, keepdims=True) / gain[...]


def stack_kernel(*refs):
    out, used = refs[-1], 0
    for part in refs[:-1]:
        out[used : used + part.shape[0], :] = part[...]
        used += part.shape[0]


def place_kernel(count, me_ref, *refs):
    sources, (rows_out, keys_out, held, chosen, sems) = refs[:count], refs[count:]
    slots, features = rows_out.shape
    width = held.shape[1]
    tag = slice(features, features + TAGS)
    spans = [tag] + [slice(k, k + STRIP) for k in range(0, features, STRIP)]
    spans += [slice(features + TAGS, width)]
    copies = []
    for k, span in enumerate(spans):
        used = 0
        copies.append([])
        for i, source in enumerate(sources):
            place = held.at[pl.ds(used, source.shape[0]), span]
            copies[k].append(pltpu.make_async_copy(source.at[:, span], place, sems.at[k, i]))
            copies[k][-1].start()
            used += source.shape[0]
    if used < held.shape[0]:
        held[used:, :] = jnp.zeros((held.shape[0] - used, width), BF16)
    for copy in copies[0]:
        copy.wait()
    tags = held[:, tag].astype(F32).T.astype(jnp.int32)
    target = jnp.where(tags[0:1] == me_ref[0] + 1, tags[1:2] * TILE + tags[2:3], -1)
    places = lax.broadcasted_iota(jnp.int32, (slots, held.shape[0]), 0)
    chosen[...] = (places == target).astype(F32).astype(BF16)
    for k, span in enumerate(spans[1:], 1):
        for copy in copies[k]:
            copy.wait()
        rows = jnp.dot(chosen[...], held[:, span], preferred_element_type=F32).astype(BF16)
        if k + 1 < len(spans):
            rows_out[:, span] = rows
        else:
            keys_out[...] = rows


def lane_sums(x):
    total = x[:, :128]
    for k in range(1, x.shape[1] // 128):
        total = total + x[:, k * 128 : (k + 1) * 128]
    return total


def over_chunks(rows, work):
    lax.fori_loop(
        0,
        rows // CHUNK,
        lambda j, carry: work(pl.ds(pl.multiple_of(j * CHUNK, CHUNK), CHUNK)) or carry,
        0,
        unroll=True,
    )


def slots_kernel(
    over_ref, rows_ref, keys_ref, w_ref, gain_ref, out_ref, w_all, grad, rows_all, sums, sems
):
    slots, features = grad.shape
    strips = [slice(k, k + STRIP) for k in range(0, features, STRIP)]
    fetches, loads, stores = [], [], []
    for i, strip in enumerate(strips):
        fetches.append(pltpu.make_async_copy(w_ref.at[strip], w_all.at[strip], sems.at[0, i]))
        here = rows_all.at[:, strip]
        loads.append(pltpu.make_async_copy(rows_ref.at[:, strip], here, sems.at[1, i]))
        stores.append(pltpu.make_async_copy(here, out_ref.at[:, strip], sems.at[2, i]))
        fetches[i].start()
        loads[i].start()
    sums[...] = jnp.zeros_like(sums)
    for i, strip in enumerate(strips):
        fetches[i].wait()
        loads[i].wait()
        grad[:, strip] = lax.dot_general(
            keys_ref[...], w_all[strip, :], (((1,), (1,)), ((), ())), preferred_element_type=F32
        )
        gain = gain_ref[:, strip]

        def add(at):
            rows = rows_all[at, strip].astype(F32)
            sums[0, at, :] += lane_sums(rows * rows)
            sums[1, at, :] += lane_sums(grad[at, strip] * gain * rows)

        over_chunks(slots, add)
    inv = lax.rsqrt(jnp.sum(sums[0], 1, keepdims=True) / features + epsilon)
    slope = jnp.sum(sums[1], 1, keepdims=True) * inv * inv * inv / features
    sums[0] = jnp.broadcast_to(inv, sums.shape[1:])
    sums[1] = jnp.broadcast_to(slope, sums.shape[1:])
    dense = over_ref[0] > 0.5
    for i, strip in enumerate(strips):
        gain = gain_ref[:, strip]

        def finish(at):
            first = jnp.concatenate([sums[0, at, :]] * (STRIP // 128), 1)
            second = jnp.concatenate([sums[1, at, :]] * (STRIP // 128), 1)
            rows = rows_all[at, strip]
            final = first * (grad[at, strip] * gain) - rows.astype(F32) * second
            rows_all[at, strip] = jnp.where(dense, rows, final.astype(BF16))

        over_chunks(slots, finish)
        stores[i].start()
    for store in stores:
        store.wait()


def output_kernel(sizes, index_ref, *refs):
    count = len(sizes)
    mine, others, out_ref = refs[:count], refs[count : 2 * count], refs[-1]
    half = mine[0].shape[1]
    step = pl.program_id(0)
    core = index_ref[sum(sizes)]
    columns = pl.ds(pl.multiple_of(core * half, half), half)
    other_columns = pl.ds(pl.multiple_of((1 - core) * half, half), half)
    first = 0
    for k, size in enumerate(sizes):

        @pl.when((step >= first) & (step < first + size))
        def _():
            out_ref[:, columns] = mine[k][...].astype(F32)
            out_ref[:, other_columns] = others[k][...].astype(F32)

        first += size


def lay_out(index, mine, others, tall, rows, filled=None):
    half = mine[0].shape[1]
    sizes = [part.shape[0] // tall for part in mine]

    def spec(k):
        first, size = sum(sizes[:k]), sizes[k]
        return pl.BlockSpec((tall, half), lambda i, ids: (jnp.clip(i - first, 0, size - 1), 0))

    specs = [spec(k) for k in range(len(sizes))]
    more = [] if filled is None else [filled]
    return pl.pallas_call(
        functools.partial(output_kernel, sizes),
        out_shape=jax.ShapeDtypeStruct((rows, 2 * half), F32),
        grid_spec=pltpu.PrefetchScalarGridSpec(
            num_scalar_prefetch=1,
            grid=(sum(sizes),),
            in_specs=specs + specs + [ANY] * len(more),
            out_specs=pl.BlockSpec((tall, 2 * half), lambda i, ids: (ids[i], 0)),
        ),
        input_output_aliases={1 + 2 * len(sizes): 0} if more else {},
        compiler_params=pltpu.CompilerParams(vmem_limit_bytes=24 << 20),
        cost_estimate=pl.CostEstimate(
            flops=0, bytes_accessed=12 * sum(sizes) * tall * half, transcendentals=0
        ),
    )(index, *mine, *others, *more)


def swap_dense(hidden, grad_keys, w_key, in_gain, dest_column, learners):
    x_float = hidden.astype(F32)
    inv_rms = lax.rsqrt(jnp.mean(x_float * x_float, -1, keepdims=True) + epsilon)
    normed = x_float * inv_rms
    grad_normed = in_gain * lax.dot_general(
        grad_keys, w_key, (((1,), (1,)), ((), ())), preferred_element_type=F32
    )
    grad_input = inv_rms * (
        grad_normed - normed * jnp.mean(grad_normed * normed, -1, keepdims=True)
    )
    onehot = (dest_column[:, None] == jnp.arange(learners, dtype=jnp.int32)[None, :]).astype(
        jnp.int32
    )
    slot_rank = jnp.sum((jnp.cumsum(onehot, 0) - onehot) * onehot, 1)
    target = dest_column * (SLOTS // learners) + slot_rank
    rows_to = (target[:, None] * TILE + jnp.arange(TILE, dtype=jnp.int32)[None, :]).reshape(-1)
    place = jnp.arange(SLOTS * TILE, dtype=jnp.int32)[:, None]
    spread = jnp.dot(
        (rows_to[None, :] == place).astype(BF16),
        grad_input.astype(BF16),
        preferred_element_type=F32,
    )
    return lax.all_to_all(spread.astype(BF16), "learn", split_axis=0, concat_axis=0, tiled=True)


def body(hidden, cotangent, importance, block_len, version, destination, w_key, in_gain, key_gain):
    learners, gens = lax.axis_size("learn"), lax.axis_size("gen")
    gen, learn = lax.axis_index("gen"), lax.axis_index("learn")
    core, across = learn % 2, (learn // 2) % 2
    capacity = SLOTS // learners
    planes = learners // 4
    packet = min(PACKET, 4 * capacity * TILE)
    passed_on = min(PASSED_ON, 2 * capacity * TILE)
    rows, features = hidden.shape
    main = rows * 3 // 4
    key_count = cotangent.shape[1]
    head = key_gain.shape[0]
    strips = features // STRIP
    blocks = 2 * gens
    width = features // blocks
    half = key_count // 2

    def limit(mebibytes):
        return pltpu.CompilerParams(vmem_limit_bytes=mebibytes << 20)


    front = packet - passed_on
    pieces = []
    for k in range(planes):
        cuts = (0, front, packet) if k == 0 else (0, packet)
        pieces += [(k * packet + low, k * packet + high) for low, high in zip(cuts, cuts[1:])]
    packed_width = features + TAGS + key_count
    steps = [(step, dy) for step in range(gens) for dy in range(2)]
    wanted = [((gen + step) % gens) * 2 + (across ^ dy) for step, dy in steps]
    in_gain_row = in_gain[None, :]
    tiles = block_len.shape[0]
    made = pl.pallas_call(
        functools.partial(
            keys_kernel, blocks, (planes, packet, passed_on, capacity), pieces
        ),
        out_shape=[jax.ShapeDtypeStruct((main, width + key_count), BF16)] * blocks
        + [jax.ShapeDtypeStruct((rows - main, width + key_count), BF16)] * blocks
        + [
            jax.ShapeDtypeStruct((high - low, packed_width), BF16) for low, high in pieces
        ]
        + [
            jax.ShapeDtypeStruct((rows, key_count), BF16),
            jax.ShapeDtypeStruct((1, 3 * head), F32),
        ],
        in_specs=[SMEM] + [ANY] * 9,
        out_specs=[VMEM] * (2 * blocks + len(pieces) + 2),
        scratch_shapes=[
            pltpu.VMEM((rows, features), BF16),
            pltpu.VMEM((1, tiles), jnp.int32),
            pltpu.VMEM((1, tiles), jnp.int32),
            pltpu.VMEM((1, rows), F32),
            pltpu.VMEM((1, tiles), jnp.int32),
            pltpu.VMEM((1, features), F32),
            pltpu.VMEM((1, head), F32),
            pltpu.VMEM((rows, key_count), BF16),
            pltpu.VMEM((features, key_count), BF16),
            pltpu.VMEM((rows, features), BF16),
            pltpu.VMEM((rows, key_count), F32),
            pltpu.VMEM((rows, 128), F32),
            pltpu.SemaphoreType.DMA((8 + strips,)),
        ],
        compiler_params=limit(KEYS_MIB),
        cost_estimate=pl.CostEstimate(
            flops=2 * rows * features * key_count, bytes_accessed=16 << 20, transcendentals=0
        ),
    )(
        jnp.stack(wanted + [learn]),
        hidden,
        block_len[None, :],
        destination[:, 0][None, :],
        importance[None, :],
        version[None, :],
        in_gain_row,
        key_gain[None, :],
        cotangent,
        w_key,
    )
    operands, rests, made = made[:blocks], made[blocks : 2 * blocks], made[2 * blocks :]
    packs, (grad_keys, sums) = made[: len(pieces)], made[len(pieces) :]

    def gather(k, operands):
        step, dy = steps[k]
        pairs = [
            (p * learners + j, ((p + step) % gens) * learners + (j ^ (2 * dy)))
            for p in range(gens)
            for j in range(learners)
        ]
        return lax.ppermute(operands[k], BOTH, pairs)

    def across_learn(part, bit):
        return swap(part, "learn", learners, bit)

    def over_y(part):
        return across_learn(part[part.shape[0] - passed_on :], 2)

    def products(part):
        keys = lax.dynamic_slice_in_dim(part, width + core * half, half, 1)
        return dot_rows(part[:, :width], keys)

    barrier = lax.optimization_barrier
    direct = [k for k, (step, dy) in enumerate(steps) if (step > 0) + dy == 1]
    diagonal = [k for k, (step, dy) in enumerate(steps) if (step > 0) + dy == 2]
    last = planes - 1
    held, passed = {0: packs[1], planes: packs[0]}, {}

    def add_products(total, parts):
        for part in parts:
            total = total + products(part) + products(across_learn(part, 1))
        return total

    bits = [4 << b for b in range(planes.bit_length() - 1)]

    def halve(total, bit):
        upper = (learn // bit) % 2
        tall = total.shape[0] // 2
        sent = lax.dynamic_slice_in_dim(total, (1 - upper) * tall, tall, 0).astype(BF16)
        kept = lax.dynamic_slice_in_dim(total, upper * tall, tall, 0)
        return kept + across_learn(sent, bit).astype(F32)

    def stack(parts):
        return pl.pallas_call(
            stack_kernel,
            out_shape=jax.ShapeDtypeStruct(
                (sum(part.shape[0] for part in parts), packed_width), BF16
            ),
            in_specs=[VMEM] * len(parts),
            out_specs=VMEM,
            compiler_params=limit(STACK_MIB),
        )(*parts)

    gathered = [gather(k, operands) for k in direct + diagonal]
    for k in range(1, last):
        held[k] = across_learn(packs[1 + k], 4 * k)
    gathered, held, packs = barrier((gathered, held, packs))

    def add_rests(state):
        parts = [rests[0]] + [gather(k, rests) for k in range(1, blocks)]
        parts += [across_learn(part, 1) for part in parts]
        total = pl.pallas_call(
            functools.partial(products_kernel, len(parts)),
            out_shape=jax.ShapeDtypeStruct((width, half), F32),
            in_specs=[SMEM] + [ANY] * len(parts),
            out_specs=VMEM,
            scratch_shapes=[
                pltpu.VMEM((len(parts), rows - main, width + key_count), BF16),
                pltpu.SemaphoreType.DMA((len(parts),)),
            ],
            compiler_params=limit(PRODUCTS_MIB),
            cost_estimate=pl.CostEstimate(flops=0, bytes_accessed=0, transcendentals=0),
        )(core[None], *parts)
        for bit in bits:
            total = halve(total, bit)
        return jnp.zeros((), F32), state[1] + total

    total = add_products(0.0, [operands[0], *gathered])
    held[last] = across_learn(packs[-1], 4 * last)
    for k in range(last):
        passed[k] = over_y(held[k])
    total, held, passed = barrier((total, held, passed))

    values = [sums]
    for k in range(1, planes):
        beside = held[k][:8, features + TAGS - head // 2 : features + TAGS].astype(F32)
        terms = beside[:6].reshape(3, head)
        flags = jnp.broadcast_to(beside[6:, :1], (2, head)).reshape(2 * head)
        values.append(jnp.concatenate([terms[0] + (terms[1] + terms[2]), flags])[None])
    while len(values) > 1:
        values = [a + b for a, b in zip(values[::2], values[1::2])]
    sums = values[0]
    for n, bit in enumerate(bits):
        total = halve(total, bit)
        if n == 0:
            stacked = stack(list(held.values()) + list(passed.values()))
            passed[last] = over_y(held[last])
            sums = butterfly_sum(sums, (("gen", gens),))
            sums = butterfly_sum(sums, (("learn", 4),), learners)
            total, passed, stacked, sums = barrier((total, passed, stacked, sums))
        if n == 1:
            stacks = [stacked, passed[last]]
            stacks += [across_learn(part, 1) for part in stacks]
            total, stacks, sums = barrier((total, stacks, sums))
    _, total = lax.while_loop(lambda state: state[0] > 0.5, add_rests, (sums[0, -1], total))

    tall = total.shape[0]
    z_place = sum(((learn // bit) % 2) * (planes >> (n + 1)) for n, bit in enumerate(bits))
    first = (gen * 2 + across) * planes + z_place
    block, gains = pl.pallas_call(
        finish_kernel,
        out_shape=[
            jax.ShapeDtypeStruct((tall, half), BF16),
            jax.ShapeDtypeStruct((1, tall), F32),
        ],
        in_specs=[SMEM, VMEM, ANY, ANY],
        out_specs=[VMEM] * 2,
        scratch_shapes=[
            pltpu.VMEM((tall, half), BF16),
            pltpu.VMEM((1, tall), F32),
            pltpu.SemaphoreType.DMA((2,)),
        ],
        compiler_params=limit(FINISH_MIB),
    )(
        jnp.stack([first, core]),
        total,
        w_key,
        lax.dynamic_slice_in_dim(in_gain, first * tall, tall)[None],
    )

    parts, y_parts, offsets = [block], [], [0]
    kgain_grad = sums[0, :head]
    place = -(-sum(part.shape[0] for part in stacks) // 128) * 128
    rows_placed, keys_placed = pl.pallas_call(
        functools.partial(place_kernel, len(stacks)),
        out_shape=[
            jax.ShapeDtypeStruct((SLOTS * TILE, features), BF16),
            jax.ShapeDtypeStruct((SLOTS * TILE, key_count), BF16),
        ],
        in_specs=[SMEM] + [ANY] * len(stacks),
        out_specs=[VMEM] * 2,
        scratch_shapes=[
            pltpu.VMEM((place, packed_width), BF16),
            pltpu.VMEM((SLOTS * TILE, place), BF16),
            pltpu.SemaphoreType.DMA((strips + 2, len(stacks))),
        ],
        compiler_params=limit(PLACE_MIB),
    )(learn[None], *stacks)
    for n, bit in enumerate(reversed(bits)):
        block = parts[0] if n == 0 else jnp.concatenate(parts, 0)
        received = across_learn(block, bit)
        y_parts.append(across_learn(parts[-1], 2))
        upper = (learn // bit) % 2
        if n + 1 == len(bits):
            near = [across_learn(gains, far) for far in (bit, 2, bit + 2)]
            gains = join_at(join(gains, near[0], upper), join(near[1], near[2], upper), across, 0)
        else:
            gains = join(gains, across_learn(gains, bit), upper)
        if n == 0:
            received, y_parts, gains, rows_placed, keys_placed = barrier(
                (received, y_parts, gains, rows_placed, keys_placed)
            )
        parts = parts + [received]
        weight = planes >> (bits.index(bit) + 1)
        offsets = offsets + [o ^ weight for o in offsets]
    _, rows_placed = lax.while_loop(
        lambda state: state[0] > 0.5,
        lambda state: (
            jnp.zeros((), F32),
            swap_dense(hidden, grad_keys, w_key, in_gain, destination[:, 0], learners),
        ),
        (sums[0, head], rows_placed),
    )
    grad_slots = pl.pallas_call(
        slots_kernel,
        out_shape=jax.ShapeDtypeStruct((SLOTS * TILE, features), BF16),
        in_specs=[SMEM, ANY, VMEM, ANY, VMEM],
        out_specs=ANY,
        scratch_shapes=[
            pltpu.VMEM((features, key_count), BF16),
            pltpu.VMEM((SLOTS * TILE, features), F32),
            pltpu.VMEM((SLOTS * TILE, features), BF16),
            pltpu.VMEM((2, SLOTS * TILE, 128), F32),
            pltpu.SemaphoreType.DMA((3, strips)),
        ],
        compiler_params=limit(SLOTS_MIB),
    )(sums[0, head : head + 1], rows_placed, keys_placed, w_key, in_gain_row)
    parts, y_parts, gains, grad_slots, kgain_grad = barrier(
        (parts, y_parts, gains, grad_slots, kgain_grad)
    )

    y_parts.append(across_learn(parts[-1], 2))
    core_parts = [across_learn(part, 1) for part in parts]
    core_y = [across_learn(part, 1) for part in y_parts[:-1]]
    first = z_place ^ jnp.asarray(offsets, jnp.int32)
    w_rows = 2 * width
    done = sum(part.shape[0] for part in y_parts[:-1]) // tall
    own_first, other_first = across * planes + first, (1 - across) * planes + first
    w_grad = lay_out(
        jnp.concatenate([own_first, other_first[:done], core[None]]),
        parts + y_parts[:-1],
        core_parts + core_y,
        tall,
        w_rows,
    )
    gains = gains + across_learn(gains, 1)
    step = 1
    while step < gens:
        gains = join(gains, swap(gains, "gen", gens, step), (gen // step) % 2)
        step *= 2
    w_grad, y_parts, gains = barrier((w_grad, y_parts, gains))
    w_grad = lay_out(
        jnp.concatenate([other_first[done:], core[None]]),
        y_parts[-1:],
        [across_learn(y_parts[-1], 1)],
        tall,
        w_rows,
        w_grad,
    )
    return (grad_slots, w_grad, gains.reshape(-1), kgain_grad)


def solution(mesh):
    return jax.shard_map(
        body,
        mesh=mesh,
        in_specs=(
            P(("gen", "learn"), None),
            P(("gen", "learn"), None),
            P(("gen", "learn")),
            P(("gen", "learn")),
            P(("gen", "learn")),
            P(("gen", "learn"), None),
            P(),
            P(),
            P(),
        ),
        out_specs=(P(("gen", "learn"), None), P("gen", None), P(), P()),
        check_vma=False,
    )
```

```python
import functools

import jax
import jax.numpy as jnp
from jax import lax
from jax.experimental import pallas as pl
from jax.experimental.pallas import tpu as pltpu
from jax.sharding import PartitionSpec as P

TILE = 8
VERSIONS = 4
SLOTS = 64
PACKET = 72
PASSED_ON = 48
TAGS = 128
STRIP = 512
UNROLL, KEYS_UNROLL = 2, 5
EXTRA = 16
CHUNK = 64
KEYS_MIB, PRODUCTS_MIB, FINISH_MIB, STACK_MIB, PLACE_MIB, SLOTS_MIB = 56, 20, 8, 20, 36, 44


epsilon = 1e-06
clip_ratio = 2.0
staleness = 0.5
BOTH = ("gen", "learn")
F32 = jnp.float32
BF16 = jnp.bfloat16


def to_column(row, size):
    same = lax.broadcasted_iota(jnp.int32, (size, size), 0) == lax.broadcasted_iota(
        jnp.int32, (size, size), 1
    )
    return jnp.sum(jnp.where(same, row, jnp.zeros_like(row)), 1, keepdims=True)


def row_values(per_block, rows):
    shape = (rows, per_block.shape[1])
    own = lax.broadcasted_iota(jnp.int32, shape, 0) // TILE == lax.broadcasted_iota(
        jnp.int32, shape, 1
    )
    return jnp.sum(jnp.where(own, per_block, jnp.zeros_like(per_block)), 1, keepdims=True)


def token_weights(importance_row, len_row, version_row):
    rows = importance_row.shape[1]
    stale_age = VERSIONS - 1 - version_row
    decay_row = jnp.zeros(stale_age.shape, F32)
    for age in range(VERSIONS):
        decay_row = jnp.where(stale_age == age, staleness**age, decay_row)
    inside = lax.broadcasted_iota(jnp.int32, (rows, 1), 0) % TILE < row_values(len_row, rows)
    importance = jnp.minimum(to_column(importance_row, rows), clip_ratio)
    return importance * (row_values(decay_row, rows) * jnp.where(inside, 1.0, 0.0))


def swap(x, axis, size, bit):
    return lax.ppermute(x, axis, [(i, i ^ bit) for i in range(size)])


def butterfly_sum(x, axes, learners=None):
    for axis, size in axes:
        bit = 1
        while bit < size:
            x = x + swap(x, axis, learners or size, bit)
            bit *= 2
    return x


def join_at(mine, other, upper, axis):
    place = lax.broadcasted_iota(jnp.int32, (2,) + (1,) * (mine.ndim - axis), 0)
    return jnp.where(
        place == upper, jnp.expand_dims(mine, axis), jnp.expand_dims(other, axis)
    )


def join(mine, other, upper):
    return join_at(mine, other, upper, 0).reshape((2 * mine.shape[0],) + mine.shape[1:])


def dot_rows(a, b):
    return lax.dot_general(a, b, (((0,), (0,)), ((), ())), preferred_element_type=F32)


VMEM = pl.BlockSpec(memory_space=pltpu.VMEM)
SMEM = pl.BlockSpec(memory_space=pltpu.SMEM)
ANY = pl.BlockSpec(memory_space=pl.ANY)


def keys_kernel(blocks, plan, pieces, index_ref, *refs):
    sources, outs, rests = refs[:9], refs[9 : 9 + blocks], refs[9 + blocks : 9 + 2 * blocks]
    refs = refs[9 + 2 * blocks :]
    main = outs[0].shape[0]
    planes, packet = plan[:2]
    packs, refs = refs[: len(pieces)], refs[len(pieces) :]
    (keys_out, sums_out), held, (w_all, h_all, keys, sums, sems) = refs[:2], refs[2:10], refs[10:]

    def spread(packed, first):
        for pack, (low, high) in zip(packs, pieces):
            pack[: high - low, first] = packed[low:high]

    w_ref = sources[8]
    copies = [
        pltpu.make_async_copy(source, place, sems.at[i])
        for i, (source, place) in enumerate(zip(sources[:8], held))
    ]
    for copy in copies:
        copy.start()
    hidden_ref, len_ref, dest_ref, importance_ref, version_ref, gain_ref, key_gain_ref = held[:7]
    cotangent_ref = held[7]
    rows, features = hidden_ref.shape
    strips = features // STRIP

    def strip(i):
        return pl.ds(pl.multiple_of(i * STRIP, STRIP), STRIP)

    def fetch(i):
        return pltpu.make_async_copy(w_ref.at[strip(i)], w_all.at[strip(i)], sems.at[8 + i])

    for i in range(strips):
        fetch(i).start()
    for copy in copies[1:3]:
        copy.wait()
    place, tags, over, order, many = packet_plan(
        index_ref[blocks], len_ref[...], dest_ref[...], rows, main, *plan
    )
    places = lax.broadcasted_iota(jnp.int32, (planes * packet, rows), 0)
    onehot = (places == place).astype(F32).astype(BF16)
    places = lax.broadcasted_iota(jnp.int32, (rows, rows), 0)
    squeeze = (places == order).astype(F32).astype(BF16)
    for copy in copies[3:]:
        copy.wait()
    weight = token_weights(importance_ref[...], len_ref[...], version_ref[...])
    copies[0].wait()

    sums[...] = jnp.zeros_like(sums)

    def squares(i, carry):
        span = strip(i)
        packed = jnp.dot(onehot, hidden_ref[:, span], preferred_element_type=F32).astype(BF16)
        spread(packed, span)

        def add(at):
            x = hidden_ref[at, span].astype(F32)
            sums[at, :] += lane_sums(x * x)

        over_chunks(rows, add)
        return carry

    lax.fori_loop(0, strips, squares, 0, unroll=KEYS_UNROLL)
    packed = jnp.dot(onehot, tags, preferred_element_type=F32).astype(BF16)
    spread(packed, slice(features, features + TAGS))
    inv = lax.rsqrt(jnp.sum(sums[...], 1, keepdims=True) / features + epsilon)
    sums[...] = jnp.broadcast_to(inv, sums.shape)
    keys[...] = jnp.zeros_like(keys)

    def project(i, carry):
        span = strip(i)
        gain = gain_ref[:, span]

        def scale(at):
            by = jnp.concatenate([sums[at, :]] * (STRIP // 128), 1)
            hidden_ref[at, span] = (hidden_ref[at, span].astype(F32) * by * gain).astype(BF16)

        over_chunks(rows, scale)
        h = hidden_ref[:, span]
        h_all[:, span] = jnp.dot(squeeze, h, preferred_element_type=F32).astype(BF16)
        fetch(i).wait()
        keys[...] += jnp.dot(h, w_all[span, :], preferred_element_type=F32)
        return carry

    lax.fori_loop(0, strips, project, 0, unroll=KEYS_UNROLL)
    width = outs[0].shape[1] - keys.shape[1]
    for k in range(blocks):
        columns = pl.ds(pl.multiple_of(index_ref[k] * width, width), width)
        outs[k][:, :width] = h_all[:main, columns]
        rests[k][:, :width] = h_all[main:, columns]
    head = key_gain_ref.shape[1]
    kgain = jnp.zeros((1, head), F32)
    for a in range(keys.shape[1] // head):
        span = slice(a * head, (a + 1) * head)
        key = keys[:, span]
        scale = lax.rsqrt(jnp.mean(key * key, 1, keepdims=True) + epsilon)
        upstream = (cotangent_ref[:, span].astype(F32) * weight).astype(BF16).astype(F32)
        kgain = kgain + jnp.sum(upstream * key * scale, 0, keepdims=True)
        scaled = upstream * key_gain_ref[...]
        grad = scale * scaled - key * (scale * scale * scale) * jnp.mean(
            scaled * key, 1, keepdims=True
        )
        keys_out[:, span] = grad.astype(BF16)
    sums_out[:, :head] = kgain
    sums_out[:, head : 2 * head] = jnp.broadcast_to(over, (1, head))
    sums_out[:, 2 * head :] = jnp.broadcast_to(many, (1, head))
    packed = jnp.dot(squeeze, keys_out[...], preferred_element_type=F32).astype(BF16)
    for k in range(blocks):
        outs[k][:, width:] = packed[:main]
        rests[k][:, width:] = packed[main:]
    packed = jnp.dot(onehot, keys_out[...], preferred_element_type=F32).astype(BF16)
    spread(packed, slice(features + TAGS, features + TAGS + keys.shape[1]))
    value = kgain
    line = lax.broadcasted_iota(jnp.int32, (EXTRA, head // 2), 0)
    split = jnp.where(line == 6, over, jnp.where(line == 7, many, 0.0))
    for i in range(3):
        term = value.astype(BF16).astype(F32)
        value = value - term
        split = jnp.where(line == 2 * i, term[:, : head // 2], split)
        split = jnp.where(line == 2 * i + 1, term[:, head // 2 :], split)
    split = jnp.concatenate([jnp.zeros((EXTRA, TAGS - head // 2), F32), split], 1)
    for pack in packs[2:]:
        beside = pack[:EXTRA, features : features + TAGS].astype(F32) + split
        pack[:EXTRA, features : features + TAGS] = beside.astype(BF16)


def packet_plan(learn, len_row, dest_row, rows, main, planes, packet, passed_on, capacity):
    tiles = dest_row.shape[1]
    dest_column = to_column(dest_row, tiles)
    shape = (tiles, tiles)
    earlier = lax.broadcasted_iota(jnp.int32, shape, 0) < lax.broadcasted_iota(jnp.int32, shape, 1)
    alike = earlier & (dest_column == dest_row)
    rank_row = jnp.sum(jnp.where(alike, 1, 0), 0, keepdims=True)
    shape = (tiles, rows)
    token = lax.broadcasted_iota(jnp.int32, shape, 1)
    own = token // TILE == lax.broadcasted_iota(jnp.int32, shape, 0)
    dest = jnp.sum(jnp.where(own, dest_column, 0), 0, keepdims=True)
    length = jnp.sum(jnp.where(own, to_column(len_row, tiles), 0), 0, keepdims=True)
    valid = token[:1] % TILE < length
    apart = dest ^ learn
    kind = jnp.where(valid, (apart // 4) * 2 + (apart // 2) % 2, 2 * planes)
    kinds = lax.broadcasted_iota(jnp.int32, (2 * planes, 1), 0)
    member = kind == kinds
    shape = (rows, rows)
    before = lax.broadcasted_iota(jnp.int32, shape, 0) < lax.broadcasted_iota(jnp.int32, shape, 1)
    counted = jnp.where(member, 1.0, 0.0)
    ahead = jnp.dot(
        counted.astype(BF16),
        jnp.where(before, 1.0, 0.0).astype(BF16),
        preferred_element_type=F32,
    ).astype(jnp.int32)
    count = jnp.sum(counted, 1, keepdims=True).astype(jnp.int32)
    start = (kinds // 2) * packet + jnp.where(kinds % 2 == 1, packet - count, 0)
    position = jnp.sum(jnp.where(member, ahead + start, 0), 0, keepdims=True)
    position = jnp.where(valid, position, -1)
    order = jnp.where(valid, jnp.sum(ahead, 0, keepdims=True), -1)
    many = jnp.where(jnp.sum(count, 0, keepdims=True) > main, 1.0, 0.0)
    plane_of = lax.broadcasted_iota(jnp.int32, (2 * planes, planes), 0) // 2
    same_plane = plane_of == lax.broadcasted_iota(jnp.int32, (2 * planes, planes), 1)
    together = jnp.sum(jnp.where(same_plane, count, 0), 0, keepdims=True)
    too_many = jnp.where((kinds % 2 == 1) & (count > passed_on), 1.0, 0.0)
    over = jnp.max(jnp.where(together > packet, 1.0, 0.0), 1, keepdims=True) + jnp.max(
        too_many, 0, keepdims=True
    )
    lane = lax.broadcasted_iota(jnp.int32, (rows, TAGS), 1)
    line = lax.broadcasted_iota(jnp.int32, (rows, TAGS), 0) % TILE
    slot = learn * capacity + row_values(rank_row, rows)
    tags = jnp.where(lane == 0, row_values(dest_row, rows) + 1, jnp.where(lane == 1, slot, line))
    tags = jnp.where(lane < 3, tags, 0)
    return position, tags.astype(F32).astype(BF16), over, order, many


def products_kernel(count, core_ref, *refs):
    sources, (out_ref, parts, sems) = refs[:count], refs[count:]
    width, half = out_ref.shape
    tall = width // 5
    keys = pl.ds(pl.multiple_of(width + core_ref[0] * half, half), half)
    copies = [
        pltpu.make_async_copy(source, parts.at[k], sems.at[k]) for k, source in enumerate(sources)
    ]
    for copy in copies:
        copy.start()
    for k, copy in enumerate(copies):
        copy.wait()

        def block(i, carry):
            rows = pl.ds(pl.multiple_of(i * tall, tall), tall)
            product = lax.dot_general(
                parts[k, :, rows],
                parts[k, :, keys],
                (((0,), (0,)), ((), ())),
                preferred_element_type=F32,
            )
            out_ref[rows, :] = product + out_ref[rows, :] if k else product
            return carry

        lax.fori_loop(0, 5, block, 0, unroll=True)


def halve_kernel(index_ref, total_ref, other_ref, sent_out, kept_out, mine, sem):
    rows = other_ref.shape[0]
    first = pl.multiple_of(index_ref[0] * rows, rows)
    copy = pltpu.make_async_copy(total_ref.at[pl.ds(first, rows)], mine, sem)
    copy.start()
    copy.wait()
    for out, place in ((sent_out, 1 - index_ref[1]), (kept_out, index_ref[1])):
        part = pl.ds(pl.multiple_of(place * (rows // 2), rows // 2), rows // 2)
        out[...] = (mine[part, :] + other_ref[part, :].astype(F32)).astype(out.dtype)


def finish_kernel(
    index_ref, kept_ref, other_ref, w_ref, gain_ref, block_out, gains_out, w_part, gain, sems
):
    tall, half = kept_ref.shape
    rows = pl.ds(pl.multiple_of(index_ref[0] * tall, tall), tall)
    columns = pl.ds(pl.multiple_of(index_ref[1] * half, half), half)
    fetch_w = pltpu.make_async_copy(w_ref.at[rows, columns], w_part, sems.at[0])
    fetch_gain = pltpu.make_async_copy(gain_ref, gain, sems.at[1])
    fetch_w.start()
    fetch_gain.start()
    total = kept_ref[...] + other_ref[...].astype(F32)
    block_out[...] = total.astype(BF16)
    fetch_gain.wait()
    fetch_w.wait()
    sums = jnp.sum(w_part[...].astype(F32) * total, 1, keepdims=True)
    shape = (tall, tall)
    same = lax.broadcasted_iota(jnp.int32, shape, 0) == lax.broadcasted_iota(jnp.int32, shape, 1)
    gains_out[...] = jnp.sum(jnp.where(same, sums, 0.0), 0, keepdims=True) / gain[...]


def stack_kernel(*refs):
    out, used = refs[-1], 0
    for part in refs[:-1]:
        out[used : used + part.shape[0], :] = part[...]
        used += part.shape[0]


def place_kernel(count, me_ref, *refs):
    sources, (rows_out, keys_out, held, chosen, sems) = refs[:count], refs[count:]
    slots, features = rows_out.shape
    width = held.shape[1]
    tag = slice(features, features + TAGS)
    spans = [tag] + [slice(k, k + STRIP) for k in range(0, features, STRIP)]
    spans += [slice(features + TAGS, width)]
    copies = []
    for k, span in enumerate(spans):
        used = 0
        copies.append([])
        for i, source in enumerate(sources):
            place = held.at[pl.ds(used, source.shape[0]), span]
            copies[k].append(pltpu.make_async_copy(source.at[:, span], place, sems.at[k, i]))
            copies[k][-1].start()
            used += source.shape[0]
    if used < held.shape[0]:
        held[used:, :] = jnp.zeros((held.shape[0] - used, width), BF16)
    for copy in copies[0]:
        copy.wait()
    tags = held[:, tag].astype(F32).T.astype(jnp.int32)
    target = jnp.where(tags[0:1] == me_ref[0] + 1, tags[1:2] * TILE + tags[2:3], -1)
    places = lax.broadcasted_iota(jnp.int32, (slots, held.shape[0]), 0)
    chosen[...] = (places == target).astype(F32).astype(BF16)
    for k, span in enumerate(spans[1:], 1):
        for copy in copies[k]:
            copy.wait()
        rows = jnp.dot(chosen[...], held[:, span], preferred_element_type=F32).astype(BF16)
        if k + 1 < len(spans):
            rows_out[:, span] = rows
        else:
            keys_out[...] = rows


def lane_sums(x):
    total = x[:, :128]
    for k in range(1, x.shape[1] // 128):
        total = total + x[:, k * 128 : (k + 1) * 128]
    return total


def over_chunks(rows, work):
    lax.fori_loop(
        0,
        rows // CHUNK,
        lambda j, carry: work(pl.ds(pl.multiple_of(j * CHUNK, CHUNK), CHUNK)) or carry,
        0,
        unroll=True,
    )


def slots_kernel(
    over_ref, rows_ref, keys_ref, w_ref, gain_ref, out_ref, w_all, grad, rows_all, sums, sems
):
    slots, features = grad.shape
    strips = features // STRIP

    def strip(i):
        return pl.ds(pl.multiple_of(i * STRIP, STRIP), STRIP)

    def fetch(i):
        return pltpu.make_async_copy(w_ref.at[strip(i)], w_all.at[strip(i)], sems.at[0, i])

    def load(i):
        here = rows_all.at[:, strip(i)]
        return pltpu.make_async_copy(rows_ref.at[:, strip(i)], here, sems.at[1, i])

    def store(i):
        here = rows_all.at[:, strip(i)]
        return pltpu.make_async_copy(here, out_ref.at[:, strip(i)], sems.at[2, i])

    for i in range(strips):
        fetch(i).start()
        load(i).start()
    sums[...] = jnp.zeros_like(sums)

    def back(i, carry):
        here = strip(i)
        fetch(i).wait()
        load(i).wait()
        grad[:, here] = lax.dot_general(
            keys_ref[...], w_all[here, :], (((1,), (1,)), ((), ())), preferred_element_type=F32
        )
        gain = gain_ref[:, here]

        def add(at):
            rows = rows_all[at, here].astype(F32)
            sums[0, at, :] += lane_sums(rows * rows)
            sums[1, at, :] += lane_sums(grad[at, here] * gain * rows)

        over_chunks(slots, add)
        return carry

    lax.fori_loop(0, strips, back, 0, unroll=UNROLL)
    inv = lax.rsqrt(jnp.sum(sums[0], 1, keepdims=True) / features + epsilon)
    slope = jnp.sum(sums[1], 1, keepdims=True) * inv * inv * inv / features
    sums[0] = jnp.broadcast_to(inv, sums.shape[1:])
    sums[1] = jnp.broadcast_to(slope, sums.shape[1:])
    dense = over_ref[0] > 0.5

    def last(i, carry):
        here = strip(i)
        gain = gain_ref[:, here]

        def finish(at):
            first = jnp.concatenate([sums[0, at, :]] * (STRIP // 128), 1)
            second = jnp.concatenate([sums[1, at, :]] * (STRIP // 128), 1)
            rows = rows_all[at, here]
            final = first * (grad[at, here] * gain) - rows.astype(F32) * second
            rows_all[at, here] = jnp.where(dense, rows, final.astype(BF16))

        over_chunks(slots, finish)
        store(i).start()
        return carry

    lax.fori_loop(0, strips, last, 0)
    for i in range(strips):
        store(i).wait()


def output_kernel(sizes, index_ref, *refs):
    count = len(sizes)
    mine, others, out_ref = refs[:count], refs[count : 2 * count], refs[-1]
    half = mine[0].shape[1]
    step = pl.program_id(0)
    core = index_ref[sum(sizes)]
    columns = pl.ds(pl.multiple_of(core * half, half), half)
    other_columns = pl.ds(pl.multiple_of((1 - core) * half, half), half)
    first = 0
    for k, size in enumerate(sizes):

        @pl.when((step >= first) & (step < first + size))
        def _():
            out_ref[:, columns] = mine[k][...].astype(F32)
            out_ref[:, other_columns] = others[k][...].astype(F32)

        first += size


def lay_out(index, mine, others, tall, rows, filled=None):
    half = mine[0].shape[1]
    sizes = [part.shape[0] // tall for part in mine]

    def spec(k):
        first, size = sum(sizes[:k]), sizes[k]
        return pl.BlockSpec((tall, half), lambda i, ids: (jnp.clip(i - first, 0, size - 1), 0))

    specs = [spec(k) for k in range(len(sizes))]
    more = [] if filled is None else [filled]
    return pl.pallas_call(
        functools.partial(output_kernel, sizes),
        out_shape=jax.ShapeDtypeStruct((rows, 2 * half), F32),
        grid_spec=pltpu.PrefetchScalarGridSpec(
            num_scalar_prefetch=1,
            grid=(sum(sizes),),
            in_specs=specs + specs + [ANY] * len(more),
            out_specs=pl.BlockSpec((tall, 2 * half), lambda i, ids: (ids[i], 0)),
        ),
        input_output_aliases={1 + 2 * len(sizes): 0} if more else {},
        compiler_params=pltpu.CompilerParams(vmem_limit_bytes=24 << 20),
        cost_estimate=pl.CostEstimate(
            flops=0, bytes_accessed=12 * sum(sizes) * tall * half, transcendentals=0
        ),
    )(index, *mine, *others, *more)


def swap_dense(hidden, grad_keys, w_key, in_gain, dest_column, learners):
    x_float = hidden.astype(F32)
    inv_rms = lax.rsqrt(jnp.mean(x_float * x_float, -1, keepdims=True) + epsilon)
    normed = x_float * inv_rms
    grad_normed = in_gain * lax.dot_general(
        grad_keys, w_key, (((1,), (1,)), ((), ())), preferred_element_type=F32
    )
    grad_input = inv_rms * (
        grad_normed - normed * jnp.mean(grad_normed * normed, -1, keepdims=True)
    )
    onehot = (dest_column[:, None] == jnp.arange(learners, dtype=jnp.int32)[None, :]).astype(
        jnp.int32
    )
    slot_rank = jnp.sum((jnp.cumsum(onehot, 0) - onehot) * onehot, 1)
    target = dest_column * (SLOTS // learners) + slot_rank
    rows_to = (target[:, None] * TILE + jnp.arange(TILE, dtype=jnp.int32)[None, :]).reshape(-1)
    place = jnp.arange(SLOTS * TILE, dtype=jnp.int32)[:, None]
    spread = jnp.dot(
        (rows_to[None, :] == place).astype(BF16),
        grad_input.astype(BF16),
        preferred_element_type=F32,
    )
    return lax.all_to_all(spread.astype(BF16), "learn", split_axis=0, concat_axis=0, tiled=True)


def body(hidden, cotangent, importance, block_len, version, destination, w_key, in_gain, key_gain):
    learners, gens = lax.axis_size("learn"), lax.axis_size("gen")
    gen, learn = lax.axis_index("gen"), lax.axis_index("learn")
    core, across = learn % 2, (learn // 2) % 2
    capacity = SLOTS // learners
    planes = learners // 4
    packet = min(PACKET, 4 * capacity * TILE)
    passed_on = min(PASSED_ON, 2 * capacity * TILE)
    rows, features = hidden.shape
    main = rows * 3 // 4
    key_count = cotangent.shape[1]
    head = key_gain.shape[0]
    strips = features // STRIP
    blocks = 2 * gens
    width = features // blocks
    half = key_count // 2

    def limit(mebibytes):
        return pltpu.CompilerParams(vmem_limit_bytes=mebibytes << 20)


    front = packet - passed_on
    pieces = []
    for k in range(planes):
        cuts = (0, front, packet) if k == 0 else (0, packet)
        pieces += [(k * packet + low, k * packet + high) for low, high in zip(cuts, cuts[1:])]
    packed_width = features + TAGS + key_count
    steps = [(step, dy) for step in range(gens) for dy in range(2)]
    wanted = [((gen + step) % gens) * 2 + (across ^ dy) for step, dy in steps]
    in_gain_row = in_gain[None, :]
    tiles = block_len.shape[0]
    made = pl.pallas_call(
        functools.partial(
            keys_kernel, blocks, (planes, packet, passed_on, capacity), pieces
        ),
        out_shape=[jax.ShapeDtypeStruct((main, width + key_count), BF16)] * blocks
        + [jax.ShapeDtypeStruct((rows - main, width + key_count), BF16)] * blocks
        + [
            jax.ShapeDtypeStruct((high - low, packed_width), BF16) for low, high in pieces
        ]
        + [
            jax.ShapeDtypeStruct((rows, key_count), BF16),
            jax.ShapeDtypeStruct((1, 3 * head), F32),
        ],
        in_specs=[SMEM] + [ANY] * 9,
        out_specs=[VMEM] * (2 * blocks + len(pieces) + 2),
        scratch_shapes=[
            pltpu.VMEM((rows, features), BF16),
            pltpu.VMEM((1, tiles), jnp.int32),
            pltpu.VMEM((1, tiles), jnp.int32),
            pltpu.VMEM((1, rows), F32),
            pltpu.VMEM((1, tiles), jnp.int32),
            pltpu.VMEM((1, features), F32),
            pltpu.VMEM((1, head), F32),
            pltpu.VMEM((rows, key_count), BF16),
            pltpu.VMEM((features, key_count), BF16),
            pltpu.VMEM((rows, features), BF16),
            pltpu.VMEM((rows, key_count), F32),
            pltpu.VMEM((rows, 128), F32),
            pltpu.SemaphoreType.DMA((8 + strips,)),
        ],
        compiler_params=limit(KEYS_MIB),
        cost_estimate=pl.CostEstimate(
            flops=2 * rows * features * key_count, bytes_accessed=16 << 20, transcendentals=0
        ),
    )(
        jnp.stack(wanted + [learn]),
        hidden,
        block_len[None, :],
        destination[:, 0][None, :],
        importance[None, :],
        version[None, :],
        in_gain_row,
        key_gain[None, :],
        cotangent,
        w_key,
    )
    operands, rests, made = made[:blocks], made[blocks : 2 * blocks], made[2 * blocks :]
    packs, (grad_keys, sums) = made[: len(pieces)], made[len(pieces) :]

    def gather(k, operands):
        step, dy = steps[k]
        pairs = [
            (p * learners + j, ((p + step) % gens) * learners + (j ^ (2 * dy)))
            for p in range(gens)
            for j in range(learners)
        ]
        return lax.ppermute(operands[k], BOTH, pairs)

    def across_learn(part, bit):
        return swap(part, "learn", learners, bit)

    def over_y(part):
        return across_learn(part[part.shape[0] - passed_on :], 2)

    def products(part):
        keys = lax.dynamic_slice_in_dim(part, width + core * half, half, 1)
        return dot_rows(part[:, :width], keys)

    barrier = lax.optimization_barrier
    direct = [k for k, (step, dy) in enumerate(steps) if (step > 0) + dy == 1]
    diagonal = [k for k, (step, dy) in enumerate(steps) if (step > 0) + dy == 2]
    last = planes - 1
    held, passed = {0: packs[1], planes: packs[0]}, {}

    bits = [4 << b for b in range(planes.bit_length() - 1)]

    def halve(total, bit):
        upper = (learn // bit) % 2
        tall = total.shape[0] // 2
        sent = lax.dynamic_slice_in_dim(total, (1 - upper) * tall, tall, 0).astype(BF16)
        kept = lax.dynamic_slice_in_dim(total, upper * tall, tall, 0)
        return kept + across_learn(sent, bit).astype(F32)

    def stack(parts):
        return pl.pallas_call(
            stack_kernel,
            out_shape=jax.ShapeDtypeStruct(
                (sum(part.shape[0] for part in parts), packed_width), BF16
            ),
            in_specs=[VMEM] * len(parts),
            out_specs=VMEM,
            compiler_params=limit(STACK_MIB),
        )(*parts)

    gathered = [gather(k, operands) for k in direct + diagonal]
    for k in range(1, last):
        held[k] = across_learn(packs[1 + k], 4 * k)
    gathered, held, packs = barrier((gathered, held, packs))

    def add_rests(state):
        parts = [rests[0]] + [gather(k, rests) for k in range(1, blocks)]
        parts += [across_learn(part, 1) for part in parts]
        total = pl.pallas_call(
            functools.partial(products_kernel, len(parts)),
            out_shape=jax.ShapeDtypeStruct((width, half), F32),
            in_specs=[SMEM] + [ANY] * len(parts),
            out_specs=VMEM,
            scratch_shapes=[
                pltpu.VMEM((len(parts), rows - main, width + key_count), BF16),
                pltpu.SemaphoreType.DMA((len(parts),)),
            ],
            compiler_params=limit(PRODUCTS_MIB),
            cost_estimate=pl.CostEstimate(flops=0, bytes_accessed=0, transcendentals=0),
        )(core[None], *parts)
        for bit in bits:
            total = halve(total, bit)
        return jnp.zeros((), F32), state[1] + total

    total = 0.0
    for part in [operands[0], *gathered]:
        total = total + products(part) + products(across_learn(part, 1))
    held[last] = across_learn(packs[-1], 4 * last)
    for k in range(last):
        passed[k] = over_y(held[k])
    total, held, passed = barrier((total, held, passed))

    values = [sums]
    for k in range(1, planes):
        beside = held[k][:8, features + TAGS - head // 2 : features + TAGS].astype(F32)
        terms = beside[:6].reshape(3, head)
        flags = jnp.broadcast_to(beside[6:, :1], (2, head)).reshape(2 * head)
        values.append(jnp.concatenate([terms[0] + (terms[1] + terms[2]), flags])[None])
    while len(values) > 1:
        values = [a + b for a, b in zip(values[::2], values[1::2])]
    sums = values[0]
    uppers = [(learn // bit) % 2 for bit in bits]
    rows_sent = width // 2
    sent = lax.dynamic_slice_in_dim(total, (1 - uppers[0]) * rows_sent, rows_sent, 0).astype(BF16)
    kept, kept_at = total, uppers[0]
    for n, bit in enumerate(bits):
        received = across_learn(sent, bit)
        if n == 0:
            stacked = stack(list(held.values()) + list(passed.values()))
            passed[last] = over_y(held[last])
            sums = butterfly_sum(sums, (("gen", gens),))
            sums = butterfly_sum(sums, (("learn", 4),), learners)
            received, kept, passed, stacked, sums = barrier(
                (received, kept, passed, stacked, sums)
            )
        if n == 1:
            stacks = [stacked, passed[last]]
            stacks += [across_learn(part, 1) for part in stacks]
        if n + 1 == len(bits):
            break
        tall = received.shape[0]
        sent, kept = pl.pallas_call(
            halve_kernel,
            out_shape=[
                jax.ShapeDtypeStruct((tall // 2, half), BF16),
                jax.ShapeDtypeStruct((tall // 2, half), F32),
            ],
            in_specs=[SMEM, ANY, VMEM],
            out_specs=[VMEM] * 2,
            scratch_shapes=[pltpu.VMEM((tall, half), F32), pltpu.SemaphoreType.DMA],
            compiler_params=limit(FINISH_MIB),
        )(jnp.stack([kept_at, uppers[n + 1]]), kept, received)
        kept_at = jnp.zeros((), jnp.int32)
    _, kept = lax.while_loop(lambda state: state[0] > 0.5, add_rests, (sums[0, -1], kept))
    received, kept, stacks, sums = barrier((received, kept, stacks, sums))

    tall = kept.shape[0]
    z_place = sum(((learn // bit) % 2) * (planes >> (n + 1)) for n, bit in enumerate(bits))
    first = (gen * 2 + across) * planes + z_place
    block, gains = pl.pallas_call(
        finish_kernel,
        out_shape=[
            jax.ShapeDtypeStruct((tall, half), BF16),
            jax.ShapeDtypeStruct((1, tall), F32),
        ],
        in_specs=[SMEM, VMEM, VMEM, ANY, ANY],
        out_specs=[VMEM] * 2,
        scratch_shapes=[
            pltpu.VMEM((tall, half), BF16),
            pltpu.VMEM((1, tall), F32),
            pltpu.SemaphoreType.DMA((2,)),
        ],
        compiler_params=limit(FINISH_MIB),
    )(
        jnp.stack([first, core]),
        kept,
        received,
        w_key,
        lax.dynamic_slice_in_dim(in_gain, first * tall, tall)[None],
    )

    parts, y_parts, offsets = [block], [], [0]
    kgain_grad = sums[0, :head]
    place = -(-sum(part.shape[0] for part in stacks) // 128) * 128
    rows_placed, keys_placed = pl.pallas_call(
        functools.partial(place_kernel, len(stacks)),
        out_shape=[
            jax.ShapeDtypeStruct((SLOTS * TILE, features), BF16),
            jax.ShapeDtypeStruct((SLOTS * TILE, key_count), BF16),
        ],
        in_specs=[SMEM] + [ANY] * len(stacks),
        out_specs=[VMEM] * 2,
        scratch_shapes=[
            pltpu.VMEM((place, packed_width), BF16),
            pltpu.VMEM((SLOTS * TILE, place), BF16),
            pltpu.SemaphoreType.DMA((strips + 2, len(stacks))),
        ],
        compiler_params=limit(PLACE_MIB),
    )(learn[None], *stacks)
    for n, bit in enumerate(reversed(bits)):
        block = parts[0] if n == 0 else jnp.concatenate(parts, 0)
        received = across_learn(block, bit)
        y_parts.append(across_learn(parts[-1], 2))
        upper = (learn // bit) % 2
        if n + 1 == len(bits):
            near = [across_learn(gains, far) for far in (bit, 2, bit + 2)]
            gains = join_at(join(gains, near[0], upper), join(near[1], near[2], upper), across, 0)
        else:
            gains = join(gains, across_learn(gains, bit), upper)
        if n == 0:
            received, y_parts, gains, rows_placed, keys_placed = barrier(
                (received, y_parts, gains, rows_placed, keys_placed)
            )
        parts = parts + [received]
        weight = planes >> (bits.index(bit) + 1)
        offsets = offsets + [o ^ weight for o in offsets]
    _, rows_placed = lax.while_loop(
        lambda state: state[0] > 0.5,
        lambda state: (
            jnp.zeros((), F32),
            swap_dense(hidden, grad_keys, w_key, in_gain, destination[:, 0], learners),
        ),
        (sums[0, head], rows_placed),
    )
    grad_slots = pl.pallas_call(
        slots_kernel,
        out_shape=jax.ShapeDtypeStruct((SLOTS * TILE, features), BF16),
        in_specs=[SMEM, ANY, VMEM, ANY, VMEM],
        out_specs=ANY,
        scratch_shapes=[
            pltpu.VMEM((features, key_count), BF16),
            pltpu.VMEM((SLOTS * TILE, features), F32),
            pltpu.VMEM((SLOTS * TILE, features), BF16),
            pltpu.VMEM((2, SLOTS * TILE, 128), F32),
            pltpu.SemaphoreType.DMA((3, strips)),
        ],
        compiler_params=limit(SLOTS_MIB),
    )(sums[0, head : head + 1], rows_placed, keys_placed, w_key, in_gain_row)
    parts, y_parts, gains, grad_slots, kgain_grad = barrier(
        (parts, y_parts, gains, grad_slots, kgain_grad)
    )

    y_parts.append(across_learn(parts[-1], 2))
    core_parts = [across_learn(part, 1) for part in parts]
    core_y = [across_learn(part, 1) for part in y_parts[:-1]]
    first = z_place ^ jnp.asarray(offsets, jnp.int32)
    w_rows = 2 * width
    done = sum(part.shape[0] for part in y_parts[:-1]) // tall
    own_first, other_first = across * planes + first, (1 - across) * planes + first
    w_grad = lay_out(
        jnp.concatenate([own_first, other_first[:done], core[None]]),
        parts + y_parts[:-1],
        core_parts + core_y,
        tall,
        w_rows,
    )
    gains = gains + across_learn(gains, 1)
    step = 1
    while step < gens:
        gains = join(gains, swap(gains, "gen", gens, step), (gen // step) % 2)
        step *= 2
    w_grad, y_parts, gains = barrier((w_grad, y_parts, gains))
    w_grad = lay_out(
        jnp.concatenate([other_first[done:], core[None]]),
        y_parts[-1:],
        [across_learn(y_parts[-1], 1)],
        tall,
        w_rows,
        w_grad,
    )
    return (grad_slots, w_grad, gains.reshape(-1), kgain_grad)


def solution(mesh):
    return jax.shard_map(
        body,
        mesh=mesh,
        in_specs=(
            P(("gen", "learn"), None),
            P(("gen", "learn"), None),
            P(("gen", "learn")),
            P(("gen", "learn")),
            P(("gen", "learn")),
            P(("gen", "learn"), None),
            P(),
            P(),
            P(),
        ),
        out_specs=(P(("gen", "learn"), None), P("gen", None), P(), P()),
        check_vma=False,
    )
```

```python
import functools

import jax
import jax.numpy as jnp
from jax import lax
from jax.experimental import pallas as pl
from jax.experimental.pallas import tpu as pltpu
from jax.sharding import PartitionSpec as P

TILE = 8
VERSIONS = 4
SLOTS = 64
PACKET = 72
PASSED_ON = 48
TAGS = 128
STRIP = 512
UNROLL, KEYS_UNROLL = 2, 10
EXTRA = 16
CHUNK = 64
KEYS_MIB, PRODUCTS_MIB, FINISH_MIB, STACK_MIB, PLACE_MIB, SLOTS_MIB = 56, 20, 8, 20, 36, 44


epsilon = 1e-06
clip_ratio = 2.0
staleness = 0.5
BOTH = ("gen", "learn")
F32 = jnp.float32
BF16 = jnp.bfloat16


def to_column(row, size):
    same = lax.broadcasted_iota(jnp.int32, (size, size), 0) == lax.broadcasted_iota(
        jnp.int32, (size, size), 1
    )
    return jnp.sum(jnp.where(same, row, jnp.zeros_like(row)), 1, keepdims=True)


def row_values(per_block, rows):
    shape = (rows, per_block.shape[1])
    own = lax.broadcasted_iota(jnp.int32, shape, 0) // TILE == lax.broadcasted_iota(
        jnp.int32, shape, 1
    )
    return jnp.sum(jnp.where(own, per_block, jnp.zeros_like(per_block)), 1, keepdims=True)


def token_weights(importance_row, len_row, version_row):
    rows = importance_row.shape[1]
    stale_age = VERSIONS - 1 - version_row
    decay_row = jnp.zeros(stale_age.shape, F32)
    for age in range(VERSIONS):
        decay_row = jnp.where(stale_age == age, staleness**age, decay_row)
    inside = lax.broadcasted_iota(jnp.int32, (rows, 1), 0) % TILE < row_values(len_row, rows)
    importance = jnp.minimum(to_column(importance_row, rows), clip_ratio)
    return importance * (row_values(decay_row, rows) * jnp.where(inside, 1.0, 0.0))


def swap(x, axis, size, bit):
    return lax.ppermute(x, axis, [(i, i ^ bit) for i in range(size)])


def butterfly_sum(x, axes, learners=None):
    for axis, size in axes:
        bit = 1
        while bit < size:
            x = x + swap(x, axis, learners or size, bit)
            bit *= 2
    return x


def join_at(mine, other, upper, axis):
    place = lax.broadcasted_iota(jnp.int32, (2,) + (1,) * (mine.ndim - axis), 0)
    return jnp.where(
        place == upper, jnp.expand_dims(mine, axis), jnp.expand_dims(other, axis)
    )


def join(mine, other, upper):
    return join_at(mine, other, upper, 0).reshape((2 * mine.shape[0],) + mine.shape[1:])


def dot_rows(a, b):
    return lax.dot_general(a, b, (((0,), (0,)), ((), ())), preferred_element_type=F32)


VMEM = pl.BlockSpec(memory_space=pltpu.VMEM)
SMEM = pl.BlockSpec(memory_space=pltpu.SMEM)
ANY = pl.BlockSpec(memory_space=pl.ANY)


def keys_kernel(blocks, plan, pieces, index_ref, *refs):
    sources, outs, rests = refs[:9], refs[9 : 9 + blocks], refs[9 + blocks : 9 + 2 * blocks]
    refs = refs[9 + 2 * blocks :]
    main = outs[0].shape[0]
    planes, packet = plan[:2]
    packs, refs = refs[: len(pieces)], refs[len(pieces) :]
    (keys_out, sums_out), held, (w_all, h_all, keys, sums, sems) = refs[:2], refs[2:10], refs[10:]

    def spread(packed, first):
        for pack, (low, high) in zip(packs, pieces):
            pack[: high - low, first] = packed[low:high]

    w_ref = sources[8]
    copies = [
        pltpu.make_async_copy(source, place, sems.at[i])
        for i, (source, place) in enumerate(zip(sources[:8], held))
    ]
    for copy in copies:
        copy.start()
    hidden_ref, len_ref, dest_ref, importance_ref, version_ref, gain_ref, key_gain_ref = held[:7]
    cotangent_ref = held[7]
    rows, features = hidden_ref.shape
    strips = features // STRIP

    def strip(i):
        return pl.ds(pl.multiple_of(i * STRIP, STRIP), STRIP)

    def fetch(i):
        return pltpu.make_async_copy(w_ref.at[strip(i)], w_all.at[strip(i)], sems.at[8 + i])

    for i in range(strips):
        fetch(i).start()
    for copy in copies[1:3]:
        copy.wait()
    place, tags, over, order, many = packet_plan(
        index_ref[blocks], len_ref[...], dest_ref[...], rows, main, *plan
    )
    places = lax.broadcasted_iota(jnp.int32, (planes * packet, rows), 0)
    onehot = (places == place).astype(F32).astype(BF16)
    places = lax.broadcasted_iota(jnp.int32, (rows, rows), 0)
    squeeze = (places == order).astype(F32).astype(BF16)
    for copy in copies[3:]:
        copy.wait()
    weight = token_weights(importance_ref[...], len_ref[...], version_ref[...])
    copies[0].wait()

    sums[...] = jnp.zeros_like(sums)

    def squares(i, carry):
        span = strip(i)
        packed = jnp.dot(onehot, hidden_ref[:, span], preferred_element_type=F32).astype(BF16)
        spread(packed, span)

        def add(at):
            x = hidden_ref[at, span].astype(F32)
            sums[at, :] += lane_sums(x * x)

        over_chunks(rows, add)
        return carry

    lax.fori_loop(0, strips, squares, 0, unroll=KEYS_UNROLL)
    packed = jnp.dot(onehot, tags, preferred_element_type=F32).astype(BF16)
    spread(packed, slice(features, features + TAGS))
    inv = lax.rsqrt(jnp.sum(sums[...], 1, keepdims=True) / features + epsilon)
    sums[...] = jnp.broadcast_to(inv, sums.shape)
    keys[...] = jnp.zeros_like(keys)

    def project(i, carry):
        span = strip(i)
        gain = gain_ref[:, span]

        def scale(at):
            by = jnp.concatenate([sums[at, :]] * (STRIP // 128), 1)
            hidden_ref[at, span] = (hidden_ref[at, span].astype(F32) * by * gain).astype(BF16)

        over_chunks(rows, scale)
        h = hidden_ref[:, span]
        h_all[:, span] = jnp.dot(squeeze, h, preferred_element_type=F32).astype(BF16)
        fetch(i).wait()
        keys[...] += jnp.dot(h, w_all[span, :], preferred_element_type=F32)
        return carry

    lax.fori_loop(0, strips, project, 0, unroll=KEYS_UNROLL)
    width = outs[0].shape[1] - keys.shape[1]
    for k in range(blocks):
        columns = pl.ds(pl.multiple_of(index_ref[k] * width, width), width)
        outs[k][:, :width] = h_all[:main, columns]
        rests[k][:, :width] = h_all[main:, columns]
    head = key_gain_ref.shape[1]
    kgain = jnp.zeros((1, head), F32)
    for a in range(keys.shape[1] // head):
        span = slice(a * head, (a + 1) * head)
        key = keys[:, span]
        scale = lax.rsqrt(jnp.mean(key * key, 1, keepdims=True) + epsilon)
        upstream = (cotangent_ref[:, span].astype(F32) * weight).astype(BF16).astype(F32)
        kgain = kgain + jnp.sum(upstream * key * scale, 0, keepdims=True)
        scaled = upstream * key_gain_ref[...]
        grad = scale * scaled - key * (scale * scale * scale) * jnp.mean(
            scaled * key, 1, keepdims=True
        )
        keys_out[:, span] = grad.astype(BF16)
    sums_out[:, :head] = kgain
    sums_out[:, head : 2 * head] = jnp.broadcast_to(over, (1, head))
    sums_out[:, 2 * head :] = jnp.broadcast_to(many, (1, head))
    packed = jnp.dot(squeeze, keys_out[...], preferred_element_type=F32).astype(BF16)
    for k in range(blocks):
        outs[k][:, width:] = packed[:main]
        rests[k][:, width:] = packed[main:]
    packed = jnp.dot(onehot, keys_out[...], preferred_element_type=F32).astype(BF16)
    spread(packed, slice(features + TAGS, features + TAGS + keys.shape[1]))
    value = kgain
    line = lax.broadcasted_iota(jnp.int32, (EXTRA, head // 2), 0)
    split = jnp.where(line == 6, over, jnp.where(line == 7, many, 0.0))
    for i in range(3):
        term = value.astype(BF16).astype(F32)
        value = value - term
        split = jnp.where(line == 2 * i, term[:, : head // 2], split)
        split = jnp.where(line == 2 * i + 1, term[:, head // 2 :], split)
    split = jnp.concatenate([jnp.zeros((EXTRA, TAGS - head // 2), F32), split], 1)
    for pack in packs[2:]:
        beside = pack[:EXTRA, features : features + TAGS].astype(F32) + split
        pack[:EXTRA, features : features + TAGS] = beside.astype(BF16)


def packet_plan(learn, len_row, dest_row, rows, main, planes, packet, passed_on, capacity):
    tiles = dest_row.shape[1]
    dest_column = to_column(dest_row, tiles)
    shape = (tiles, tiles)
    earlier = lax.broadcasted_iota(jnp.int32, shape, 0) < lax.broadcasted_iota(jnp.int32, shape, 1)
    alike = earlier & (dest_column == dest_row)
    rank_row = jnp.sum(jnp.where(alike, 1, 0), 0, keepdims=True)
    shape = (tiles, rows)
    token = lax.broadcasted_iota(jnp.int32, shape, 1)
    own = token // TILE == lax.broadcasted_iota(jnp.int32, shape, 0)
    dest = jnp.sum(jnp.where(own, dest_column, 0), 0, keepdims=True)
    length = jnp.sum(jnp.where(own, to_column(len_row, tiles), 0), 0, keepdims=True)
    valid = token[:1] % TILE < length
    apart = dest ^ learn
    kind = jnp.where(valid, (apart // 4) * 2 + (apart // 2) % 2, 2 * planes)
    kinds = lax.broadcasted_iota(jnp.int32, (2 * planes, 1), 0)
    member = kind == kinds
    shape = (rows, rows)
    before = lax.broadcasted_iota(jnp.int32, shape, 0) < lax.broadcasted_iota(jnp.int32, shape, 1)
    counted = jnp.where(member, 1.0, 0.0)
    ahead = jnp.dot(
        counted.astype(BF16),
        jnp.where(before, 1.0, 0.0).astype(BF16),
        preferred_element_type=F32,
    ).astype(jnp.int32)
    count = jnp.sum(counted, 1, keepdims=True).astype(jnp.int32)
    start = (kinds // 2) * packet + jnp.where(kinds % 2 == 1, packet - count, 0)
    position = jnp.sum(jnp.where(member, ahead + start, 0), 0, keepdims=True)
    position = jnp.where(valid, position, -1)
    order = jnp.where(valid, jnp.sum(ahead, 0, keepdims=True), -1)
    many = jnp.where(jnp.sum(count, 0, keepdims=True) > main, 1.0, 0.0)
    plane_of = lax.broadcasted_iota(jnp.int32, (2 * planes, planes), 0) // 2
    same_plane = plane_of == lax.broadcasted_iota(jnp.int32, (2 * planes, planes), 1)
    together = jnp.sum(jnp.where(same_plane, count, 0), 0, keepdims=True)
    too_many = jnp.where((kinds % 2 == 1) & (count > passed_on), 1.0, 0.0)
    over = jnp.max(jnp.where(together > packet, 1.0, 0.0), 1, keepdims=True) + jnp.max(
        too_many, 0, keepdims=True
    )
    lane = lax.broadcasted_iota(jnp.int32, (rows, TAGS), 1)
    line = lax.broadcasted_iota(jnp.int32, (rows, TAGS), 0) % TILE
    slot = learn * capacity + row_values(rank_row, rows)
    tags = jnp.where(lane == 0, row_values(dest_row, rows) + 1, jnp.where(lane == 1, slot, line))
    tags = jnp.where(lane < 3, tags, 0)
    return position, tags.astype(F32).astype(BF16), over, order, many


def products_kernel(count, core_ref, *refs):
    sources, (out_ref, parts, sems) = refs[:count], refs[count:]
    width, half = out_ref.shape
    tall = width // 5
    keys = pl.ds(pl.multiple_of(width + core_ref[0] * half, half), half)
    copies = [
        pltpu.make_async_copy(source, parts.at[k], sems.at[k]) for k, source in enumerate(sources)
    ]
    for copy in copies:
        copy.start()
    for k, copy in enumerate(copies):
        copy.wait()

        def block(i, carry):
            rows = pl.ds(pl.multiple_of(i * tall, tall), tall)
            product = lax.dot_general(
                parts[k, :, rows],
                parts[k, :, keys],
                (((0,), (0,)), ((), ())),
                preferred_element_type=F32,
            )
            out_ref[rows, :] = product + out_ref[rows, :] if k else product
            return carry

        lax.fori_loop(0, 5, block, 0, unroll=True)


def halve_kernel(index_ref, total_ref, other_ref, sent_out, kept_out, mine, sem):
    rows = other_ref.shape[0]
    first = pl.multiple_of(index_ref[0] * rows, rows)
    copy = pltpu.make_async_copy(total_ref.at[pl.ds(first, rows)], mine, sem)
    copy.start()
    copy.wait()
    for out, place in ((sent_out, 1 - index_ref[1]), (kept_out, index_ref[1])):
        part = pl.ds(pl.multiple_of(place * (rows // 2), rows // 2), rows // 2)
        out[...] = (mine[part, :] + other_ref[part, :].astype(F32)).astype(out.dtype)


def finish_kernel(
    index_ref, kept_ref, other_ref, w_ref, gain_ref, block_out, gains_out, w_part, gain, sems
):
    tall, half = kept_ref.shape
    rows = pl.ds(pl.multiple_of(index_ref[0] * tall, tall), tall)
    columns = pl.ds(pl.multiple_of(index_ref[1] * half, half), half)
    fetch_w = pltpu.make_async_copy(w_ref.at[rows, columns], w_part, sems.at[0])
    fetch_gain = pltpu.make_async_copy(gain_ref, gain, sems.at[1])
    fetch_w.start()
    fetch_gain.start()
    total = kept_ref[...] + other_ref[...].astype(F32)
    block_out[...] = total.astype(BF16)
    fetch_gain.wait()
    fetch_w.wait()
    sums = jnp.sum(w_part[...].astype(F32) * total, 1, keepdims=True)
    shape = (tall, tall)
    same = lax.broadcasted_iota(jnp.int32, shape, 0) == lax.broadcasted_iota(jnp.int32, shape, 1)
    gains_out[...] = jnp.sum(jnp.where(same, sums, 0.0), 0, keepdims=True) / gain[...]


def stack_kernel(*refs):
    out, used = refs[-1], 0
    for part in refs[:-1]:
        out[used : used + part.shape[0], :] = part[...]
        used += part.shape[0]


def place_kernel(count, me_ref, *refs):
    sources, (rows_out, keys_out, held, chosen, sems) = refs[:count], refs[count:]
    slots, features = rows_out.shape
    width = held.shape[1]
    tag = slice(features, features + TAGS)
    spans = [tag] + [slice(k, k + STRIP) for k in range(0, features, STRIP)]
    spans += [slice(features + TAGS, width)]
    copies = []
    for k, span in enumerate(spans):
        used = 0
        copies.append([])
        for i, source in enumerate(sources):
            place = held.at[pl.ds(used, source.shape[0]), span]
            copies[k].append(pltpu.make_async_copy(source.at[:, span], place, sems.at[k, i]))
            copies[k][-1].start()
            used += source.shape[0]
    if used < held.shape[0]:
        held[used:, :] = jnp.zeros((held.shape[0] - used, width), BF16)
    for copy in copies[0]:
        copy.wait()
    tags = held[:, tag].astype(F32).T.astype(jnp.int32)
    target = jnp.where(tags[0:1] == me_ref[0] + 1, tags[1:2] * TILE + tags[2:3], -1)
    places = lax.broadcasted_iota(jnp.int32, (slots, held.shape[0]), 0)
    chosen[...] = (places == target).astype(F32).astype(BF16)
    for k, span in enumerate(spans[1:], 1):
        for copy in copies[k]:
            copy.wait()
        rows = jnp.dot(chosen[...], held[:, span], preferred_element_type=F32).astype(BF16)
        if k + 1 < len(spans):
            rows_out[:, span] = rows
        else:
            keys_out[...] = rows


def lane_sums(x):
    total = x[:, :128]
    for k in range(1, x.shape[1] // 128):
        total = total + x[:, k * 128 : (k + 1) * 128]
    return total


def over_chunks(rows, work):
    lax.fori_loop(
        0,
        rows // CHUNK,
        lambda j, carry: work(pl.ds(pl.multiple_of(j * CHUNK, CHUNK), CHUNK)) or carry,
        0,
        unroll=True,
    )


def slots_kernel(
    over_ref, rows_ref, keys_ref, w_ref, gain_ref, out_ref, w_all, grad, rows_all, sums, sems
):
    slots, features = grad.shape
    strips = features // STRIP

    def strip(i):
        return pl.ds(pl.multiple_of(i * STRIP, STRIP), STRIP)

    def fetch(i):
        return pltpu.make_async_copy(w_ref.at[strip(i)], w_all.at[strip(i)], sems.at[0, i])

    def load(i):
        here = rows_all.at[:, strip(i)]
        return pltpu.make_async_copy(rows_ref.at[:, strip(i)], here, sems.at[1, i])

    def store(i):
        here = rows_all.at[:, strip(i)]
        return pltpu.make_async_copy(here, out_ref.at[:, strip(i)], sems.at[2, i])

    for i in range(strips):
        fetch(i).start()
        load(i).start()
    sums[...] = jnp.zeros_like(sums)

    def back(i, carry):
        here = strip(i)
        fetch(i).wait()
        load(i).wait()
        grad[:, here] = lax.dot_general(
            keys_ref[...], w_all[here, :], (((1,), (1,)), ((), ())), preferred_element_type=F32
        )
        gain = gain_ref[:, here]

        def add(at):
            rows = rows_all[at, here].astype(F32)
            sums[0, at, :] += lane_sums(rows * rows)
            sums[1, at, :] += lane_sums(grad[at, here] * gain * rows)

        over_chunks(slots, add)
        return carry

    lax.fori_loop(0, strips, back, 0, unroll=UNROLL)
    inv = lax.rsqrt(jnp.sum(sums[0], 1, keepdims=True) / features + epsilon)
    slope = jnp.sum(sums[1], 1, keepdims=True) * inv * inv * inv / features
    sums[0] = jnp.broadcast_to(inv, sums.shape[1:])
    sums[1] = jnp.broadcast_to(slope, sums.shape[1:])
    dense = over_ref[0] > 0.5

    def last(i, carry):
        here = strip(i)
        gain = gain_ref[:, here]

        def finish(at):
            first = jnp.concatenate([sums[0, at, :]] * (STRIP // 128), 1)
            second = jnp.concatenate([sums[1, at, :]] * (STRIP // 128), 1)
            rows = rows_all[at, here]
            final = first * (grad[at, here] * gain) - rows.astype(F32) * second
            rows_all[at, here] = jnp.where(dense, rows, final.astype(BF16))

        over_chunks(slots, finish)
        store(i).start()
        return carry

    lax.fori_loop(0, strips, last, 0)
    for i in range(strips):
        store(i).wait()


def output_kernel(sizes, index_ref, *refs):
    count = len(sizes)
    mine, others, out_ref = refs[:count], refs[count : 2 * count], refs[-1]
    half = mine[0].shape[1]
    step = pl.program_id(0)
    core = index_ref[sum(sizes)]
    columns = pl.ds(pl.multiple_of(core * half, half), half)
    other_columns = pl.ds(pl.multiple_of((1 - core) * half, half), half)
    first = 0
    for k, size in enumerate(sizes):

        @pl.when((step >= first) & (step < first + size))
        def _():
            out_ref[:, columns] = mine[k][...].astype(F32)
            out_ref[:, other_columns] = others[k][...].astype(F32)

        first += size


def lay_out(index, mine, others, tall, rows, filled=None):
    half = mine[0].shape[1]
    sizes = [part.shape[0] // tall for part in mine]

    def spec(k):
        first, size = sum(sizes[:k]), sizes[k]
        return pl.BlockSpec((tall, half), lambda i, ids: (jnp.clip(i - first, 0, size - 1), 0))

    specs = [spec(k) for k in range(len(sizes))]
    more = [] if filled is None else [filled]
    return pl.pallas_call(
        functools.partial(output_kernel, sizes),
        out_shape=jax.ShapeDtypeStruct((rows, 2 * half), F32),
        grid_spec=pltpu.PrefetchScalarGridSpec(
            num_scalar_prefetch=1,
            grid=(sum(sizes),),
            in_specs=specs + specs + [ANY] * len(more),
            out_specs=pl.BlockSpec((tall, 2 * half), lambda i, ids: (ids[i], 0)),
        ),
        input_output_aliases={1 + 2 * len(sizes): 0} if more else {},
        compiler_params=pltpu.CompilerParams(vmem_limit_bytes=24 << 20),
        cost_estimate=pl.CostEstimate(
            flops=0, bytes_accessed=12 * sum(sizes) * tall * half, transcendentals=0
        ),
    )(index, *mine, *others, *more)


def swap_dense(hidden, grad_keys, w_key, in_gain, dest_column, learners):
    x_float = hidden.astype(F32)
    inv_rms = lax.rsqrt(jnp.mean(x_float * x_float, -1, keepdims=True) + epsilon)
    normed = x_float * inv_rms
    grad_normed = in_gain * lax.dot_general(
        grad_keys, w_key, (((1,), (1,)), ((), ())), preferred_element_type=F32
    )
    grad_input = inv_rms * (
        grad_normed - normed * jnp.mean(grad_normed * normed, -1, keepdims=True)
    )
    onehot = (dest_column[:, None] == jnp.arange(learners, dtype=jnp.int32)[None, :]).astype(
        jnp.int32
    )
    slot_rank = jnp.sum((jnp.cumsum(onehot, 0) - onehot) * onehot, 1)
    target = dest_column * (SLOTS // learners) + slot_rank
    rows_to = (target[:, None] * TILE + jnp.arange(TILE, dtype=jnp.int32)[None, :]).reshape(-1)
    place = jnp.arange(SLOTS * TILE, dtype=jnp.int32)[:, None]
    spread = jnp.dot(
        (rows_to[None, :] == place).astype(BF16),
        grad_input.astype(BF16),
        preferred_element_type=F32,
    )
    return lax.all_to_all(spread.astype(BF16), "learn", split_axis=0, concat_axis=0, tiled=True)


def body(hidden, cotangent, importance, block_len, version, destination, w_key, in_gain, key_gain):
    learners, gens = lax.axis_size("learn"), lax.axis_size("gen")
    gen, learn = lax.axis_index("gen"), lax.axis_index("learn")
    core, across = learn % 2, (learn // 2) % 2
    capacity = SLOTS // learners
    planes = learners // 4
    packet = min(PACKET, 4 * capacity * TILE)
    passed_on = min(PASSED_ON, 2 * capacity * TILE)
    rows, features = hidden.shape
    main = rows * 3 // 4
    key_count = cotangent.shape[1]
    head = key_gain.shape[0]
    strips = features // STRIP
    blocks = 2 * gens
    width = features // blocks
    half = key_count // 2

    def limit(mebibytes):
        return pltpu.CompilerParams(vmem_limit_bytes=mebibytes << 20)


    front = packet - passed_on
    pieces = []
    for k in range(planes):
        cuts = (0, front, packet) if k == 0 else (0, packet)
        pieces += [(k * packet + low, k * packet + high) for low, high in zip(cuts, cuts[1:])]
    packed_width = features + TAGS + key_count
    steps = [(step, dy) for step in range(gens) for dy in range(2)]
    wanted = [((gen + step) % gens) * 2 + (across ^ dy) for step, dy in steps]
    in_gain_row = in_gain[None, :]
    tiles = block_len.shape[0]
    made = pl.pallas_call(
        functools.partial(
            keys_kernel, blocks, (planes, packet, passed_on, capacity), pieces
        ),
        out_shape=[jax.ShapeDtypeStruct((main, width + key_count), BF16)] * blocks
        + [jax.ShapeDtypeStruct((rows - main, width + key_count), BF16)] * blocks
        + [
            jax.ShapeDtypeStruct((high - low, packed_width), BF16) for low, high in pieces
        ]
        + [
            jax.ShapeDtypeStruct((rows, key_count), BF16),
            jax.ShapeDtypeStruct((1, 3 * head), F32),
        ],
        in_specs=[SMEM] + [ANY] * 9,
        out_specs=[VMEM] * (2 * blocks + len(pieces) + 2),
        scratch_shapes=[
            pltpu.VMEM((rows, features), BF16),
            pltpu.VMEM((1, tiles), jnp.int32),
            pltpu.VMEM((1, tiles), jnp.int32),
            pltpu.VMEM((1, rows), F32),
            pltpu.VMEM((1, tiles), jnp.int32),
            pltpu.VMEM((1, features), F32),
            pltpu.VMEM((1, head), F32),
            pltpu.VMEM((rows, key_count), BF16),
            pltpu.VMEM((features, key_count), BF16),
            pltpu.VMEM((rows, features), BF16),
            pltpu.VMEM((rows, key_count), F32),
            pltpu.VMEM((rows, 128), F32),
            pltpu.SemaphoreType.DMA((8 + strips,)),
        ],
        compiler_params=limit(KEYS_MIB),
        cost_estimate=pl.CostEstimate(
            flops=2 * rows * features * key_count, bytes_accessed=16 << 20, transcendentals=0
        ),
    )(
        jnp.stack(wanted + [learn]),
        hidden,
        block_len[None, :],
        destination[:, 0][None, :],
        importance[None, :],
        version[None, :],
        in_gain_row,
        key_gain[None, :],
        cotangent,
        w_key,
    )
    operands, rests, made = made[:blocks], made[blocks : 2 * blocks], made[2 * blocks :]
    packs, (grad_keys, sums) = made[: len(pieces)], made[len(pieces) :]

    def gather(k, operands):
        step, dy = steps[k]
        pairs = [
            (p * learners + j, ((p + step) % gens) * learners + (j ^ (2 * dy)))
            for p in range(gens)
            for j in range(learners)
        ]
        return lax.ppermute(operands[k], BOTH, pairs)

    def across_learn(part, bit):
        return swap(part, "learn", learners, bit)

    def over_y(part):
        return across_learn(part[part.shape[0] - passed_on :], 2)

    def products(part):
        keys = lax.dynamic_slice_in_dim(part, width + core * half, half, 1)
        return dot_rows(part[:, :width], keys)

    barrier = lax.optimization_barrier
    direct = [k for k, (step, dy) in enumerate(steps) if (step > 0) + dy == 1]
    diagonal = [k for k, (step, dy) in enumerate(steps) if (step > 0) + dy == 2]
    last = planes - 1
    held, passed = {0: packs[1], planes: packs[0]}, {}

    bits = [4 << b for b in range(planes.bit_length() - 1)]

    def halve(total, bit):
        upper = (learn // bit) % 2
        tall = total.shape[0] // 2
        sent = lax.dynamic_slice_in_dim(total, (1 - upper) * tall, tall, 0).astype(BF16)
        kept = lax.dynamic_slice_in_dim(total, upper * tall, tall, 0)
        return kept + across_learn(sent, bit).astype(F32)

    def stack(parts):
        return pl.pallas_call(
            stack_kernel,
            out_shape=jax.ShapeDtypeStruct(
                (sum(part.shape[0] for part in parts), packed_width), BF16
            ),
            in_specs=[VMEM] * len(parts),
            out_specs=VMEM,
            compiler_params=limit(STACK_MIB),
        )(*parts)

    gathered = [gather(k, operands) for k in direct + diagonal]
    for k in range(1, last):
        held[k] = across_learn(packs[1 + k], 4 * k)
    gathered, held, packs = barrier((gathered, held, packs))

    def add_rests(state):
        parts = [rests[0]] + [gather(k, rests) for k in range(1, blocks)]
        parts += [across_learn(part, 1) for part in parts]
        total = pl.pallas_call(
            functools.partial(products_kernel, len(parts)),
            out_shape=jax.ShapeDtypeStruct((width, half), F32),
            in_specs=[SMEM] + [ANY] * len(parts),
            out_specs=VMEM,
            scratch_shapes=[
                pltpu.VMEM((len(parts), rows - main, width + key_count), BF16),
                pltpu.SemaphoreType.DMA((len(parts),)),
            ],
            compiler_params=limit(PRODUCTS_MIB),
            cost_estimate=pl.CostEstimate(flops=0, bytes_accessed=0, transcendentals=0),
        )(core[None], *parts)
        for bit in bits:
            total = halve(total, bit)
        return jnp.zeros((), F32), state[1] + total

    held[last] = across_learn(packs[-1], 4 * last)
    for k in range(last):
        passed[k] = over_y(held[k])
    total = 0.0
    for part in [operands[0], *gathered]:
        total = total + products(part) + products(across_learn(part, 1))
    total, held, passed = barrier((total, held, passed))

    values = [sums]
    for k in range(1, planes):
        beside = held[k][:8, features + TAGS - head // 2 : features + TAGS].astype(F32)
        terms = beside[:6].reshape(3, head)
        flags = jnp.broadcast_to(beside[6:, :1], (2, head)).reshape(2 * head)
        values.append(jnp.concatenate([terms[0] + (terms[1] + terms[2]), flags])[None])
    while len(values) > 1:
        values = [a + b for a, b in zip(values[::2], values[1::2])]
    sums = values[0]
    uppers = [(learn // bit) % 2 for bit in bits]
    rows_sent = width // 2
    sent = lax.dynamic_slice_in_dim(total, (1 - uppers[0]) * rows_sent, rows_sent, 0).astype(BF16)
    kept, kept_at = total, uppers[0]
    for n, bit in enumerate(bits):
        received = across_learn(sent, bit)
        if n == 0:
            stacked = stack(list(held.values()) + list(passed.values()))
            passed[last] = over_y(held[last])
            sums = butterfly_sum(sums, (("gen", gens),))
            sums = butterfly_sum(sums, (("learn", 4),), learners)
            received, kept, passed, stacked, sums = barrier(
                (received, kept, passed, stacked, sums)
            )
        if n == 1:
            stacks = [stacked, passed[last]]
            stacks += [across_learn(part, 1) for part in stacks]
        if n + 1 == len(bits):
            break
        tall = received.shape[0]
        sent, kept = pl.pallas_call(
            halve_kernel,
            out_shape=[
                jax.ShapeDtypeStruct((tall // 2, half), BF16),
                jax.ShapeDtypeStruct((tall // 2, half), F32),
            ],
            in_specs=[SMEM, ANY, VMEM],
            out_specs=[VMEM] * 2,
            scratch_shapes=[pltpu.VMEM((tall, half), F32), pltpu.SemaphoreType.DMA],
            compiler_params=limit(FINISH_MIB),
        )(jnp.stack([kept_at, uppers[n + 1]]), kept, received)
        kept_at = jnp.zeros((), jnp.int32)
    _, kept = lax.while_loop(lambda state: state[0] > 0.5, add_rests, (sums[0, -1], kept))
    received, kept, stacks, sums = barrier((received, kept, stacks, sums))

    tall = kept.shape[0]
    z_place = sum(((learn // bit) % 2) * (planes >> (n + 1)) for n, bit in enumerate(bits))
    first = (gen * 2 + across) * planes + z_place
    block, gains = pl.pallas_call(
        finish_kernel,
        out_shape=[
            jax.ShapeDtypeStruct((tall, half), BF16),
            jax.ShapeDtypeStruct((1, tall), F32),
        ],
        in_specs=[SMEM, VMEM, VMEM, ANY, ANY],
        out_specs=[VMEM] * 2,
        scratch_shapes=[
            pltpu.VMEM((tall, half), BF16),
            pltpu.VMEM((1, tall), F32),
            pltpu.SemaphoreType.DMA((2,)),
        ],
        compiler_params=limit(FINISH_MIB),
    )(
        jnp.stack([first, core]),
        kept,
        received,
        w_key,
        lax.dynamic_slice_in_dim(in_gain, first * tall, tall)[None],
    )

    parts, y_parts, offsets = [block], [], [0]
    kgain_grad = sums[0, :head]
    place = -(-sum(part.shape[0] for part in stacks) // 128) * 128
    rows_placed, keys_placed = pl.pallas_call(
        functools.partial(place_kernel, len(stacks)),
        out_shape=[
            jax.ShapeDtypeStruct((SLOTS * TILE, features), BF16),
            jax.ShapeDtypeStruct((SLOTS * TILE, key_count), BF16),
        ],
        in_specs=[SMEM] + [ANY] * len(stacks),
        out_specs=[VMEM] * 2,
        scratch_shapes=[
            pltpu.VMEM((place, packed_width), BF16),
            pltpu.VMEM((SLOTS * TILE, place), BF16),
            pltpu.SemaphoreType.DMA((strips + 2, len(stacks))),
        ],
        compiler_params=limit(PLACE_MIB),
    )(learn[None], *stacks)
    for n, bit in enumerate(reversed(bits)):
        block = parts[0] if n == 0 else jnp.concatenate(parts, 0)
        received = across_learn(block, bit)
        y_parts.append(across_learn(parts[-1], 2))
        upper = (learn // bit) % 2
        if n + 1 == len(bits):
            near = [across_learn(gains, far) for far in (bit, 2, bit + 2)]
            gains = join_at(join(gains, near[0], upper), join(near[1], near[2], upper), across, 0)
        else:
            gains = join(gains, across_learn(gains, bit), upper)
        if n == 0:
            received, y_parts, gains, rows_placed, keys_placed = barrier(
                (received, y_parts, gains, rows_placed, keys_placed)
            )
        parts = parts + [received]
        weight = planes >> (bits.index(bit) + 1)
        offsets = offsets + [o ^ weight for o in offsets]
    _, rows_placed = lax.while_loop(
        lambda state: state[0] > 0.5,
        lambda state: (
            jnp.zeros((), F32),
            swap_dense(hidden, grad_keys, w_key, in_gain, destination[:, 0], learners),
        ),
        (sums[0, head], rows_placed),
    )
    grad_slots = pl.pallas_call(
        slots_kernel,
        out_shape=jax.ShapeDtypeStruct((SLOTS * TILE, features), BF16),
        in_specs=[SMEM, ANY, VMEM, ANY, VMEM],
        out_specs=ANY,
        scratch_shapes=[
            pltpu.VMEM((features, key_count), BF16),
            pltpu.VMEM((SLOTS * TILE, features), F32),
            pltpu.VMEM((SLOTS * TILE, features), BF16),
            pltpu.VMEM((2, SLOTS * TILE, 128), F32),
            pltpu.SemaphoreType.DMA((3, strips)),
        ],
        compiler_params=limit(SLOTS_MIB),
    )(sums[0, head : head + 1], rows_placed, keys_placed, w_key, in_gain_row)
    parts, y_parts, gains, grad_slots, kgain_grad = barrier(
        (parts, y_parts, gains, grad_slots, kgain_grad)
    )

    y_parts.append(across_learn(parts[-1], 2))
    core_parts = [across_learn(part, 1) for part in parts]
    core_y = [across_learn(part, 1) for part in y_parts[:-1]]
    first = z_place ^ jnp.asarray(offsets, jnp.int32)
    w_rows = 2 * width
    done = sum(part.shape[0] for part in y_parts[:-1]) // tall
    own_first, other_first = across * planes + first, (1 - across) * planes + first
    w_grad = lay_out(
        jnp.concatenate([own_first, other_first[:done], core[None]]),
        parts + y_parts[:-1],
        core_parts + core_y,
        tall,
        w_rows,
    )
    gains = gains + across_learn(gains, 1)
    step = 1
    while step < gens:
        gains = join(gains, swap(gains, "gen", gens, step), (gen // step) % 2)
        step *= 2
    w_grad, y_parts, gains = barrier((w_grad, y_parts, gains))
    w_grad = lay_out(
        jnp.concatenate([other_first[done:], core[None]]),
        y_parts[-1:],
        [across_learn(y_parts[-1], 1)],
        tall,
        w_rows,
        w_grad,
    )
    return (grad_slots, w_grad, gains.reshape(-1), kgain_grad)


def solution(mesh):
    return jax.shard_map(
        body,
        mesh=mesh,
        in_specs=(
            P(("gen", "learn"), None),
            P(("gen", "learn"), None),
            P(("gen", "learn")),
            P(("gen", "learn")),
            P(("gen", "learn")),
            P(("gen", "learn"), None),
            P(),
            P(),
            P(),
        ),
        out_specs=(P(("gen", "learn"), None), P("gen", None), P(), P()),
        check_vma=False,
    )
```
